32 devices in a mesh: rep: 4 (over y, x), shard: 8 (over z, core).
Axes of the slice: x: 2, y: 2, z: 4, core: 2. Of those that a mesh axis runs over, the one named last changes fastest.
Arguments:
- queries: bfloat16 [4, 1024, 2048], P('rep', 'shard'), may hold values from -6 to 6
- keys: bfloat16 [4, 1024, 256], P('rep', 'shard'), may hold values from -6 to 6
- values: bfloat16 [4, 1024, 256], P('rep', 'shard'), may hold values from -6 to 6
- segments: int32 [4, 1024], P('rep', 'shard'), may hold values from 0 to 15, never falling along the last dimension, each value on 1 to 512 neighbouring positions
- grad_output: bfloat16 [4, 1024, 1024], P('rep', 'shard'), may hold values from -0.375 to 0.375
Outputs:
- attention: bfloat16 [4, 1024, 2048], P('rep', 'shard')
- grad_weight: float32 [1024, 2048], P('shard')
The draws below stay inside these ranges and needn't reach their ends.
Inputs may be any that keep to these rules, and one draw needn't show every extreme that they name: `segments`: document numbers never fall along a packed row; every document holds 1 to 512 positions and some document holds exactly 512.
All inputs are finite; a program needn't handle non-finite values.
Results may differ from the reference program's by a relative error of at most 0.015.
Values may be sent and summed in bfloat16 or wider, within the bound.
A program may use at most 64 MiB of HBM per device.

```python
import math
import jax
import jax.numpy as jnp
import numpy as np
from jax import lax

HEADS = 16
KVH = 2
HD = 128
D_WIN = 1024
TOK_DEV = 128
MOST = 512
SEQ = 1024
BATCH = 4
DOCS = 16
N_SHARD = 8


def draw_queries(key, part):
    shape_full = (BATCH, SEQ, HEADS * HD)
    base = jax.random.normal(jax.random.fold_in(key, 22), shape_full, jnp.float32)
    return jnp.clip(base, -6.0, 6.0).astype(jnp.bfloat16)


def draw_keys(key, part):
    shape_full = (BATCH, SEQ, KVH * HD)
    base = jax.random.normal(jax.random.fold_in(key, 32), shape_full, jnp.float32)
    return jnp.clip(base, -6.0, 6.0).astype(jnp.bfloat16)


def with_spikes(drawn, stream_key, source, target, blocks, factor):
    owner, partner = [(jnp.arange(drawn.shape[axis_at]) // (drawn.shape[axis_at] // blocks)).reshape([-1 if axis == axis_at else 1 for axis in range(drawn.ndim)]) for axis_at in (source, target)]
    chosen = jax.random.permutation(stream_key, blocks)[partner]
    strong = (owner == chosen) | (owner == (partner + blocks // 2) % blocks)
    return jnp.where(strong, factor * drawn, drawn)


def shard_levels(rng, dims, split, least, largest):
    def one(axis_at, shards_of):
        draws = jax.random.uniform(jax.random.fold_in(jax.random.fold_in(rng, 6), axis_at), (shards_of,), jnp.float32, least / len(split), largest / len(split))
        return jnp.repeat(jnp.exp(draws), dims[axis_at] // shards_of).reshape((-1,) + (1,) * (len(dims) - axis_at - 1))

    gain = one(*split[0])
    for cut in split[1:]:
        gain = gain * one(*cut)
    return gain


def length_profile(amount, total, reach, lean):
    portions = [(1 << 20) // math.isqrt(standing ** lean) + 1 for standing in range(2, amount + 1)]
    rest, given = total - reach - (amount - 1), [1] * (amount - 1)
    while rest > 0:
        movable = [i for i in range(amount - 1) if given[i] < reach]
        mass, left = sum([portions[i] for i in movable]), rest
        for i in movable:
            extra = min(reach - given[i], max(1, left * portions[i] // mass), rest)
            given[i] = given[i] + extra
            rest = rest - extra
    return np.array([reach] + given)


def ragged(stream_key, count, total, reach, lean):
    if count == 2:
        one = jax.random.randint(stream_key, (), max(1, total - reach), min(reach, total - 1) + 1)
        return jnp.stack([one, total - one])
    tallies = jnp.asarray(length_profile(count, total, reach, lean), jnp.int32)
    couples = (count - 1) // 2
    source_of, receiver = tallies[1:1 + 2 * couples:2], tallies[2:2 + 2 * couples:2]
    margin = jnp.minimum(source_of - 1, reach - receiver)
    passed = jax.random.randint(jax.random.fold_in(stream_key, 1), (couples,), 0, 1 << 20) % (margin + 1)
    tallies = tallies.at[1:1 + 2 * couples:2].set(source_of - passed).at[2:2 + 2 * couples:2].set(receiver + passed)
    return tallies[jax.random.permutation(jax.random.fold_in(stream_key, 2), count)]


def centred(key, dims, deviation, most, split=(), kind=jnp.bfloat16):
    result = jax.random.normal(key, dims, jnp.float32) * deviation
    if len(split) > 0:
        result = shard_levels(key, dims, split, -0.22, 0.18) * result
    return jnp.clip(result, min=-most, max=most).astype(kind)


def bell_draw_with(stream_key, shape, width, limit, pieces, heavy, kind=jnp.bfloat16):
    entries = width * jax.random.normal(stream_key, shape, jnp.float32)
    if pieces:
        entries = entries * shard_levels(stream_key, shape, pieces, -0.22, 0.18)
    return jnp.clip(with_spikes(entries, jax.random.fold_in(stream_key, 3), *heavy), -limit, limit).astype(kind)


def setup_inputs(seed: int = 0) -> dict:
    splits = jax.random.split(jax.random.key(seed), 6)
    queries = draw_queries(jax.random.fold_in(splits[5], 71), 0)
    keys = draw_keys(jax.random.fold_in(splits[5], 71), 0)
    values = centred(splits[2], (BATCH, SEQ, KVH * HD), 1.0, 6.0, ((0, 4), (1, 8)))
    segments = jax.vmap(lambda own: jnp.searchsorted(jnp.cumsum(ragged(own, DOCS, SEQ, MOST, 2)), jnp.arange(SEQ), side="right"))(jax.random.split(splits[3], BATCH)).reshape((BATCH, SEQ)).astype(jnp.int32)
    grad_output = bell_draw_with(splits[4], (BATCH, SEQ, D_WIN), (3.0 / (BATCH * SEQ) ** 0.5), 0.375, ((0, 4), (1, 8)), (1, 2, 8, 2.0))
    return dict(queries=queries, keys=keys, values=values, segments=segments, grad_output=grad_output)


def attend_row(queries_row, keys_row, values_row, segment_row):
    block_rows = min(512, SEQ)
    window = min(block_rows + MOST, SEQ)
    group_size = HEADS // KVH

    def one_block(block_index):
        q_first = (block_index * block_rows).astype(jnp.int32)
        k_first = jnp.clip(q_first + block_rows - window, 0, SEQ - window).astype(jnp.int32)
        q_block = lax.dynamic_slice_in_dim(queries_row, q_first, block_rows, 0).astype(jnp.float32)
        q_block = q_block.reshape(block_rows, KVH, group_size, HD)
        k_block = lax.dynamic_slice_in_dim(keys_row, k_first, window, 0).astype(jnp.float32).reshape(window, KVH, HD)
        v_block = lax.dynamic_slice_in_dim(values_row, k_first, window, 0).astype(jnp.float32).reshape(window, KVH, HD)
        q_seg = lax.dynamic_slice_in_dim(segment_row, q_first, block_rows, 0)
        k_seg = lax.dynamic_slice_in_dim(segment_row, k_first, window, 0)
        q_pos = q_first + jnp.arange(block_rows, dtype=jnp.int32)
        k_pos = k_first + jnp.arange(window, dtype=jnp.int32)
        allowed = (q_seg[:, None] == k_seg[None, :]) & (k_pos[None, :] <= q_pos[:, None])
        scores = jnp.einsum("qhgd,khd->hgqk", q_block, k_block) * (HD ** -0.5)
        scores = jnp.where(allowed, scores, -1e30)
        row_max = jnp.max(scores, axis=-1, keepdims=True)
        weights = jnp.where(allowed, jnp.exp(scores - row_max), 0.0)
        denominator = jnp.sum(weights, axis=-1)
        mixed = jnp.einsum("hgqk,khd->hgqd", weights, v_block, precision=lax.Precision.HIGHEST)
        mixed = mixed / denominator[..., None]
        output_rows = jnp.transpose(mixed, (2, 0, 1, 3)).reshape(block_rows, HEADS * HD)
        return output_rows.astype(jnp.bfloat16)

    blocks = lax.map(one_block, jnp.arange(SEQ // block_rows, dtype=jnp.int32))
    return blocks.reshape(SEQ, HEADS * HD)


def row_attention(row_data):
    return attend_row(*row_data)


def reference(queries, keys, values, segments, grad_output):
    attention = lax.map(row_attention, (queries, keys, values, segments))
    flat_attn = attention.reshape(BATCH * N_SHARD, TOK_DEV, HEADS * HD)
    flat_grad = grad_output.reshape(BATCH * N_SHARD, TOK_DEV, D_WIN)

    def add_block(running, pair):
        partial_value = lax.dot_general(pair[1], pair[0], (((0,), (0,)), ((), ())), preferred_element_type=jnp.float32)
        rounded = lax.optimization_barrier(partial_value.astype(jnp.bfloat16))
        return running + rounded.astype(jnp.float32), None

    grad_weight, unused = lax.scan(add_block, jnp.zeros((D_WIN, HEADS * HD), jnp.float32), (flat_attn, flat_grad))
    return attention, grad_weight
```

```python
import functools

import jax
import jax.numpy as jnp
from jax import lax
from jax.experimental import pallas as pl
from jax.experimental.pallas import tpu as pltpu
from jax.sharding import PartitionSpec as P

HEADS = 16
KVH = 2
HD = 128
MOST = 512
MESH = pl.DeviceIdType.MESH
F32 = jnp.float32
BF16 = jnp.bfloat16
SCALE = HD ** (-0.5) * 1.4426950408889634


def kernel(
    n_rep, n_shard,
    q_ref, k_ref, v_ref, seg_ref, g_ref,
    attn_ref, gw_ref,
    kv, kext, vext, bias, gt_out, gt, a_all, p_out, z_in, o_all,
    zk_send, zk_recv, sb_send, sb_recv, g_send, g_recv, a_send, a_recv,
    p_send, p_recv, o_send, o_recv,
):
    rows = q_ref.shape[0]
    span = MOST // rows
    reach = span // 2
    n_chip = n_shard // 2
    out_rows = g_ref.shape[1] // n_shard
    heads_each = HEADS // n_rep
    width = heads_each * HD
    rep = lax.axis_index("rep")
    me = lax.axis_index("shard")
    core = lax.rem(me, 2)
    chip = me // 2
    sib = me + 1 - 2 * core
    other = 1 - core
    slot = rep * 2 + core
    sib_slot = rep * 2 + other

    def remote(src, dst, send_sem, recv_sem, to_rep, to_shard):
        return pltpu.make_async_remote_copy(
            src_ref=src, dst_ref=dst, send_sem=send_sem, recv_sem=recv_sem,
            device_id=(to_rep, to_shard), device_id_type=MESH,
        )

    def rep_at(step):
        return lax.rem(rep + step, n_rep)

    def chip_at(step):
        return lax.rem(chip + step, n_chip)

    barrier = pltpu.get_barrier_semaphore()
    pl.semaphore_signal(barrier, inc=1, device_id=(rep, sib), device_id_type=MESH)
    for step in range(1, n_chip):
        pl.semaphore_signal(
            barrier, inc=1, device_id=(rep, chip_at(step) * 2 + core), device_id_type=MESH
        )
    for step in range(1, n_rep):
        for side in range(2):
            pl.semaphore_signal(
                barrier, inc=1, device_id=(rep_at(step), chip * 2 + side), device_id_type=MESH
            )
    seg_row = seg_ref[...].astype(F32)
    kv[span, 0:rows, 0:KVH * HD] = k_ref[...]
    kv[span, 0:rows, KVH * HD:2 * KVH * HD] = v_ref[...]
    kv[span, rows:rows + 16, :] = jnp.zeros((16, 2 * KVH * HD), BF16)
    kv[span, rows:rows + 16, 0:rows] = jnp.broadcast_to(seg_row, (16, rows)).astype(BF16)
    for place in range(span):
        @pl.when(me - span + place < 0)
        def _(place=place):
            kv[place] = jnp.zeros(kv.shape[1:], BF16)
    pl.semaphore_wait(barrier, 1 + (n_chip - 1) + 2 * (n_rep - 1))

    def along(d):
        return remote(
            kv.at[span], kv.at[span - 2 * d], zk_send.at[d - 1], zk_recv.at[d - 1],
            rep, me + 2 * d,
        )

    for d in range(1, reach + 1):
        @pl.when(chip + d < n_chip)
        def _(d=d):
            along(d).start()

    def across(d):
        place = span + 1 - 2 * d
        return remote(
            kv.at[place + 1 - 2 * core], kv.at[place], sb_send.at[d - 1], sb_recv.at[d - 1],
            rep, sib,
        )

    def across_exists(d):
        return sib - 2 * d + 1 >= 0

    @pl.when(core == 0)
    def _():
        across(1).start()

    for b in range(n_shard):
        if (b * out_rows) % 128 == 0:
            take = max(out_rows, 128)
            piece = g_ref[:, b * out_rows:b * out_rows + take].astype(F32).T.astype(BF16)
        lead = (b * out_rows) % 128 if out_rows < 128 else 0
        gt_out[b % 2, (b // 2) * out_rows:(b // 2 + 1) * out_rows, :] = piece[lead:lead + out_rows]

    def g_copy(step, side):
        return remote(
            gt_out.at[side], gt.at[:, pl.ds(pl.multiple_of(slot * rows, 128), rows)],
            g_send.at[2 * step + side], g_recv.at[slot], rep_at(step), chip * 2 + side,
        )

    for step in range(1, n_rep):
        for side in range(2):
            g_copy(step, side).start()
    g_sib = remote(
        gt_out.at[other], gt.at[:, pl.ds(pl.multiple_of(slot * rows, 128), rows)],
        g_send.at[0], g_recv.at[slot], rep, sib,
    )
    g_sib.start()
    gt[:, pl.ds(pl.multiple_of(slot * rows, 128), rows)] = gt_out[core]

    for d in range(1, reach + 1):
        @pl.when(chip >= d)
        def _(d=d):
            along(d).wait_recv()
        if d <= reach:
            @pl.when((core == 1) & across_exists(d))
            def _(d=d):
                across(d).start()
        if d + 1 <= reach:
            @pl.when((core == 0) & across_exists(d + 1))
            def _(d=d):
                across(d + 1).start()
    for d in range(1, reach + 1):
        @pl.when(me - 2 * d + 1 >= 0)
        def _(d=d):
            across(d).wait_recv()

    q_seg = jnp.broadcast_to(seg_row, (rows, rows)).T
    for place in range(span + 1):
        k_seg = kv[place, rows:rows + 16, 0:rows].astype(F32)[0:1]
        allowed = q_seg == k_seg
        if place == span:
            q_at = lax.broadcasted_iota(jnp.int32, (rows, rows), 0)
            k_at = lax.broadcasted_iota(jnp.int32, (rows, rows), 1)
            allowed = allowed & (k_at <= q_at)
        else:
            block = lax.broadcasted_iota(jnp.int32, (rows, rows), 0) * 0 + (me - span + place)
            allowed = allowed & (block >= 0)
        bias[:, place * rows:(place + 1) * rows] = jnp.where(allowed, 0.0, -1e30)
        for head in range(KVH):
            lo = head * HD
            span_rows = slice(place * rows, (place + 1) * rows)
            kext[head, span_rows, :] = kv[place, 0:rows, lo:lo + HD]
            vext[head, span_rows, 0:HD] = kv[place, 0:rows, KVH * HD + lo:KVH * HD + lo + HD]
            vext[head, span_rows, HD:2 * HD] = jnp.ones((rows, HD), BF16)

    def columns(step):
        return pl.ds(pl.multiple_of(rep_at(step) * width, 128), width)

    def a_copy(step, side):
        return remote(
            attn_ref.at[:, columns(step)], a_all.at[pl.ds(slot * rows, rows), :],
            a_send.at[2 * step + side], a_recv.at[slot], rep_at(step), chip * 2 + side,
        )

    a_sib = remote(
        attn_ref.at[:, columns(0)], a_all.at[pl.ds(slot * rows, rows), :],
        a_send.at[0], a_recv.at[slot], rep, sib,
    )
    for step in list(range(1, n_rep)) + [0]:
        for j in range(heads_each):
            head = rep_at(step) * heads_each + j
            group = head // (HEADS // KVH)
            lanes = pl.ds(pl.multiple_of(head * HD, 128), HD)
            s = lax.dot_general(
                q_ref[:, lanes], kext[group], (((1,), (1,)), ((), ())),
                preferred_element_type=F32,
            ) + bias[...]
            top = jnp.max(s, axis=-1, keepdims=True)
            p = jnp.exp2((s - top) * SCALE).astype(BF16)
            o = jnp.dot(p, vext[group], preferred_element_type=F32)
            mixed = (o[:, 0:HD] / o[:, HD:2 * HD]).astype(BF16)
            attn_ref[:, lanes] = mixed
            if step == 0:
                a_all[pl.ds(slot * rows, rows), j * HD:(j + 1) * HD] = mixed
        if step == 0:
            a_sib.start()
        else:
            for side in range(2):
                a_copy(step, side).start()

    def arrived(index):
        remote(
            gt_out.at[0], gt.at[:, pl.ds(pl.multiple_of(index * rows, 128), rows)],
            g_send.at[0], g_recv.at[index], rep, sib,
        ).wait_recv()
        remote(
            attn_ref.at[:, columns(0)], a_all.at[pl.ds(index * rows, rows), :],
            a_send.at[0], a_recv.at[index], rep, sib,
        ).wait_recv()

    arrived(sib_slot)
    for step in range(1, n_rep):
        for side in range(2):
            arrived(rep_at(n_rep - step) * 2 + side)

    def term(target):
        block = gt[pl.ds(pl.multiple_of(target * out_rows, 16), out_rows), :]
        return jnp.dot(block, a_all[...], preferred_element_type=F32)

    def p_copy(step):
        return remote(
            p_out.at[chip_at(step)], z_in.at[chip], p_send.at[step], p_recv.at[chip],
            rep, chip_at(step) * 2 + core,
        )

    for step in range(1, n_chip):
        p_out[chip_at(step)] = term(chip_at(step)).astype(BF16)
        p_copy(step).start()
    total = term(chip)
    for step in range(1, n_chip):
        source = chip_at(n_chip - step)
        remote(
            p_out.at[0], z_in.at[source], p_send.at[0], p_recv.at[source], rep, sib
        ).wait_recv()
        total = total + z_in[source].astype(F32)

    o_all[rep] = total.astype(BF16)

    def o_copy(step):
        return remote(
            o_all.at[rep], o_all.at[rep], o_send.at[step], o_recv.at[rep], rep_at(step), me
        )

    for step in range(1, n_rep):
        o_copy(step).start()
    gw_ref[:, columns(0)] = o_all[rep].astype(F32)
    for step in range(1, n_rep):
        source = rep_at(n_rep - step)
        remote(
            o_all.at[source], o_all.at[source], o_send.at[0], o_recv.at[source], rep, sib
        ).wait_recv()
        gw_ref[:, columns(n_rep - step)] = o_all[source].astype(F32)

    for d in range(1, reach + 1):
        @pl.when(chip + d < n_chip)
        def _(d=d):
            along(d).wait_send()

        @pl.when(across_exists(d))
        def _(d=d):
            across(d).wait_send()
    g_sib.wait_send()
    a_sib.wait_send()
    for step in range(1, n_rep):
        for side in range(2):
            g_copy(step, side).wait_send()
            a_copy(step, side).wait_send()
        o_copy(step).wait_send()
    for step in range(1, n_chip):
        p_copy(step).wait_send()


def local(queries, keys, values, segments, grad_output):
    n_rep, n_shard = lax.axis_size("rep"), lax.axis_size("shard")
    rows = queries.shape[1]
    span = MOST // rows
    reach = span // 2
    n_chip = n_shard // 2
    features = grad_output.shape[2]
    out_rows = features // n_shard
    width = HEADS * HD // n_rep
    vmem = pl.BlockSpec(memory_space=pltpu.VMEM)
    dma = pltpu.SemaphoreType.DMA
    attn, grad_weight = pl.pallas_call(
        functools.partial(kernel, n_rep, n_shard),
        out_shape=(
            jax.ShapeDtypeStruct((rows, HEADS * HD), BF16),
            jax.ShapeDtypeStruct((out_rows, HEADS * HD), F32),
        ),
        in_specs=[vmem] * 5,
        out_specs=(vmem, vmem),
        scratch_shapes=[
            pltpu.VMEM((span + 1, rows + 16, 2 * KVH * HD), BF16),
            pltpu.VMEM((KVH, (span + 1) * rows, HD), BF16),
            pltpu.VMEM((KVH, (span + 1) * rows, 2 * HD), BF16),
            pltpu.VMEM((rows, (span + 1) * rows), F32),
            pltpu.VMEM((2, features // 2, rows), BF16),
            pltpu.VMEM((features // 2, 2 * n_rep * rows), BF16),
            pltpu.VMEM((2 * n_rep * rows, width), BF16),
            pltpu.VMEM((n_chip, out_rows, width), BF16),
            pltpu.VMEM((n_chip, out_rows, width), BF16),
            pltpu.VMEM((n_rep, out_rows, width), BF16),
            dma((reach,)), dma((reach,)), dma((reach,)), dma((reach,)),
            dma((2 * n_rep,)), dma((2 * n_rep,)), dma((2 * n_rep,)), dma((2 * n_rep,)),
            dma((n_chip,)), dma((n_chip,)), dma((n_rep,)), dma((n_rep,)),
        ],
        compiler_params=pltpu.CompilerParams(
            collective_id=0, has_side_effects=True, vmem_limit_bytes=40 * 1024 * 1024
        ),
    )(queries[0], keys[0], values[0], segments, grad_output[0])
    return attn[None], grad_weight


def solution(mesh):
    placed = (
        P("rep", "shard", None),
        P("rep", "shard", None),
        P("rep", "shard", None),
        P("rep", "shard"),
        P("rep", "shard", None),
    )
    return jax.shard_map(
        local,
        mesh=mesh,
        in_specs=placed,
        out_specs=(P("rep", "shard", None), P("shard", None)),
        check_vma=False,
    )
```

```python
import functools

import jax
import jax.numpy as jnp
from jax import lax
from jax.experimental import pallas as pl
from jax.experimental.pallas import tpu as pltpu
from jax.sharding import PartitionSpec as P

HEADS = 16
KVH = 2
HD = 128
MOST = 512
MESH = pl.DeviceIdType.MESH
EARLY = 4
F32 = jnp.float32
BF16 = jnp.bfloat16
SCALE = HD ** (-0.5) * 1.4426950408889634


def kernel_narrow(
    n_rep, n_shard,
    q_hbm, k_hbm, v_hbm, seg_hbm, g_hbm,
    attn_ref, gw_ref,
    q_ref, seg_ref, g_ref, in_sem, kv, kext, vext, bias, gt_out, gt, a_all, p_out, z_in, o_all,
    zk_send, zk_recv, sb_send, sb_recv, g_send, g_recv, a_send, a_recv,
    p_send, p_recv, o_send, o_recv,
):
    rows = q_ref.shape[0]
    half = KVH * HD
    span = MOST // rows
    reach = span // 2
    n_chip = n_shard // 2
    out_rows = g_ref.shape[1] // n_shard
    heads_each = HEADS // n_rep
    width = heads_each * HD
    rep = lax.axis_index("rep")
    me = lax.axis_index("shard")
    core = lax.rem(me, 2)
    chip = me // 2
    sib = me + 1 - 2 * core
    other = 1 - core
    slot = rep * 2 + core
    sib_slot = rep * 2 + other

    def remote(src, dst, send_sem, recv_sem, to_rep, to_shard):
        return pltpu.make_async_remote_copy(
            src_ref=src, dst_ref=dst, send_sem=send_sem, recv_sem=recv_sem,
            device_id=(to_rep, to_shard), device_id_type=MESH,
        )

    def rep_at(step):
        return lax.rem(rep + step, n_rep)

    def chip_at(step):
        return lax.rem(chip + step, n_chip)

    loads = [
        pltpu.make_async_copy(src, dst, in_sem.at[i])
        for i, (src, dst) in enumerate([
            (k_hbm, kv.at[span, 0:rows, 0:half]),
            (v_hbm, kv.at[span, 0:rows, half:2 * half]),
            (seg_hbm, seg_ref),
            (g_hbm, g_ref),
            (q_hbm, q_ref),
        ])
    ]
    for load in loads:
        load.start()

    barrier = pltpu.get_barrier_semaphore()
    pl.semaphore_signal(barrier, inc=1, device_id=(rep, sib), device_id_type=MESH)
    for step in range(1, n_chip):
        pl.semaphore_signal(
            barrier, inc=1, device_id=(rep, chip_at(step) * 2 + core), device_id_type=MESH
        )
    for step in range(1, n_rep):
        for side in range(2):
            pl.semaphore_signal(
                barrier, inc=1, device_id=(rep_at(step), chip * 2 + side), device_id_type=MESH
            )
    for place in range(span):
        @pl.when(me - span + place < 0)
        def _(place=place):
            kv[place] = jnp.zeros(kv.shape[1:], BF16)
    kv[span, rows:rows + 16, :] = jnp.zeros((16, 2 * half), BF16)
    for load in loads[:3]:
        load.wait()
    seg_row = seg_ref[...].astype(F32)
    kv[span, rows:rows + 16, 0:rows] = jnp.broadcast_to(seg_row, (16, rows)).astype(BF16)
    pl.semaphore_wait(barrier, 1 + (n_chip - 1) + 2 * (n_rep - 1))

    def along(d):
        return remote(
            kv.at[span], kv.at[span - 2 * d], zk_send.at[d - 1], zk_recv.at[d - 1],
            rep, me + 2 * d,
        )

    for d in range(1, reach + 1):
        @pl.when(chip + d < n_chip)
        def _(d=d):
            along(d).start()

    def across(d):
        place = span + 1 - 2 * d
        return remote(
            kv.at[place + 1 - 2 * core], kv.at[place], sb_send.at[d - 1], sb_recv.at[d - 1],
            rep, sib,
        )

    def across_exists(d):
        return sib - 2 * d + 1 >= 0

    @pl.when(core == 0)
    def _():
        across(1).start()

    loads[3].wait()

    for b in range(n_shard):
        if (b * out_rows) % 128 == 0:
            take = max(out_rows, 128)
            piece = g_ref[:, b * out_rows:b * out_rows + take].astype(F32).T.astype(BF16)
        lead = (b * out_rows) % 128 if out_rows < 128 else 0
        gt_out[b % 2, (b // 2) * out_rows:(b // 2 + 1) * out_rows, :] = piece[lead:lead + out_rows]

    def g_copy(step, side):
        return remote(
            gt_out.at[side], gt.at[:, pl.ds(pl.multiple_of(slot * rows, 128), rows)],
            g_send.at[2 * step + side], g_recv.at[slot], rep_at(step), chip * 2 + side,
        )

    for step in range(1, n_rep):
        for side in range(2):
            g_copy(step, side).start()
    g_sib = remote(
        gt_out.at[other], gt.at[:, pl.ds(pl.multiple_of(slot * rows, 128), rows)],
        g_send.at[0], g_recv.at[slot], rep, sib,
    )
    g_sib.start()
    gt[:, pl.ds(pl.multiple_of(slot * rows, 128), rows)] = gt_out[core]

    for d in range(1, reach + 1):
        @pl.when(chip >= d)
        def _(d=d):
            along(d).wait_recv()
        if d <= reach:
            @pl.when((core == 1) & across_exists(d))
            def _(d=d):
                across(d).start()
        if d + 1 <= reach:
            @pl.when((core == 0) & across_exists(d + 1))
            def _(d=d):
                across(d + 1).start()
    for d in range(1, reach + 1):
        @pl.when(me - 2 * d + 1 >= 0)
        def _(d=d):
            across(d).wait_recv()

    q_seg = jnp.broadcast_to(seg_row, (rows, rows)).T
    for place in range(span + 1):
        k_seg = kv[place, rows:rows + 16, 0:rows].astype(F32)[0:1]
        allowed = q_seg == k_seg
        if place == span:
            q_at = lax.broadcasted_iota(jnp.int32, (rows, rows), 0)
            k_at = lax.broadcasted_iota(jnp.int32, (rows, rows), 1)
            allowed = allowed & (k_at <= q_at)
        else:
            block = lax.broadcasted_iota(jnp.int32, (rows, rows), 0) * 0 + (me - span + place)
            allowed = allowed & (block >= 0)
        bias[:, place * rows:(place + 1) * rows] = jnp.where(allowed, 0.0, -1e30)
        for head in range(KVH):
            lo = head * HD
            span_rows = slice(place * rows, (place + 1) * rows)
            kext[head, span_rows, :] = kv[place, 0:rows, lo:lo + HD]
            vext[head, span_rows, 0:HD] = kv[place, 0:rows, KVH * HD + lo:KVH * HD + lo + HD]
            vext[head, span_rows, HD:2 * HD] = jnp.ones((rows, HD), BF16)

    loads[4].wait()

    def columns(step):
        return pl.ds(pl.multiple_of(rep_at(step) * width, 128), width)

    def a_copy(step, side):
        return remote(
            attn_ref.at[:, columns(step)], a_all.at[pl.ds(slot * rows, rows), :],
            a_send.at[2 * step + side], a_recv.at[slot], rep_at(step), chip * 2 + side,
        )

    a_sib = remote(
        attn_ref.at[:, columns(0)], a_all.at[pl.ds(slot * rows, rows), :],
        a_send.at[0], a_recv.at[slot], rep, sib,
    )
    for step in list(range(1, n_rep)) + [0]:
        for j in range(heads_each):
            head = rep_at(step) * heads_each + j
            group = head // (HEADS // KVH)
            lanes = pl.ds(pl.multiple_of(head * HD, 128), HD)
            s = lax.dot_general(
                q_ref[:, lanes], kext[group], (((1,), (1,)), ((), ())),
                preferred_element_type=F32,
            ) + bias[...]
            top = jnp.max(s, axis=-1, keepdims=True)
            p = jnp.exp2((s - top) * SCALE).astype(BF16)
            o = jnp.dot(p, vext[group], preferred_element_type=F32)
            mixed = (o[:, 0:HD] / o[:, HD:2 * HD]).astype(BF16)
            attn_ref[:, lanes] = mixed
            if step == 0:
                a_all[pl.ds(slot * rows, rows), j * HD:(j + 1) * HD] = mixed
        if step == 0:
            a_sib.start()
        else:
            for side in range(2):
                a_copy(step, side).start()

    def arrived(index):
        remote(
            gt_out.at[0], gt.at[:, pl.ds(pl.multiple_of(index * rows, 128), rows)],
            g_send.at[0], g_recv.at[index], rep, sib,
        ).wait_recv()
        remote(
            attn_ref.at[:, columns(0)], a_all.at[pl.ds(index * rows, rows), :],
            a_send.at[0], a_recv.at[index], rep, sib,
        ).wait_recv()

    arrived(sib_slot)
    for step in range(1, n_rep):
        for side in range(2):
            arrived(rep_at(n_rep - step) * 2 + side)

    def term(target):
        block = gt[pl.ds(pl.multiple_of(target * out_rows, 16), out_rows), :]
        return jnp.dot(block, a_all[...], preferred_element_type=F32)

    def p_copy(step):
        return remote(
            p_out.at[chip_at(step)], z_in.at[chip], p_send.at[step], p_recv.at[chip],
            rep, chip_at(step) * 2 + core,
        )

    for step in range(1, n_chip):
        p_out[chip_at(step)] = term(chip_at(step)).astype(BF16)
        p_copy(step).start()
    total = term(chip)
    for step in range(1, n_chip):
        source = chip_at(n_chip - step)
        remote(
            p_out.at[0], z_in.at[source], p_send.at[0], p_recv.at[source], rep, sib
        ).wait_recv()
        total = total + z_in[source].astype(F32)

    o_all[rep] = total.astype(BF16)

    def o_copy(step):
        return remote(
            o_all.at[rep], o_all.at[rep], o_send.at[step], o_recv.at[rep], rep_at(step), me
        )

    for step in range(1, n_rep):
        o_copy(step).start()
    gw_ref[:, columns(0)] = o_all[rep].astype(F32)
    for step in range(1, n_rep):
        source = rep_at(n_rep - step)
        remote(
            o_all.at[source], o_all.at[source], o_send.at[0], o_recv.at[source], rep, sib
        ).wait_recv()
        gw_ref[:, columns(n_rep - step)] = o_all[source].astype(F32)

    for d in range(1, reach + 1):
        @pl.when(chip + d < n_chip)
        def _(d=d):
            along(d).wait_send()

        @pl.when(across_exists(d))
        def _(d=d):
            across(d).wait_send()
    g_sib.wait_send()
    a_sib.wait_send()
    for step in range(1, n_rep):
        for side in range(2):
            g_copy(step, side).wait_send()
            a_copy(step, side).wait_send()
        o_copy(step).wait_send()
    for step in range(1, n_chip):
        p_copy(step).wait_send()


def kernel(
    n_rep, n_shard,
    q_hbm, k_hbm, v_hbm, seg_hbm, g_hbm,
    attn_hbm, gw_ref,
    q_ref, seg_ref, g_ref, in_sem, kv, kext, vext, bias, gt_out, gt, attn_vm, a_all, p_out, z_in, o_all,
    zk_send, zk_recv, sb_send, sb_recv, g_send, g_recv, a_send, a_recv,
    p_send, p_recv, o_send, o_recv, f_send, out_sem,
):
    rows = q_ref.shape[0]
    half = KVH * HD
    span = MOST // rows
    reach = span // 2
    n_chip = n_shard // 2
    out_rows = g_ref.shape[1] // n_shard
    heads_each = HEADS // n_rep
    halves = heads_each // 2
    slots = 2 * n_rep
    rep = lax.axis_index("rep")
    me = lax.axis_index("shard")
    core = lax.rem(me, 2)
    chip = me // 2
    sib = me + 1 - 2 * core
    other = 1 - core
    slot = rep * 2 + core
    sib_slot = rep * 2 + other

    def remote(src, dst, send_sem, recv_sem, to_rep, to_shard):
        return pltpu.make_async_remote_copy(
            src_ref=src, dst_ref=dst, send_sem=send_sem, recv_sem=recv_sem,
            device_id=(to_rep, to_shard), device_id_type=MESH,
        )

    def rep_at(step):
        return lax.rem(rep + step, n_rep)

    loads = [
        pltpu.make_async_copy(src, dst, in_sem.at[i])
        for i, (src, dst) in enumerate([
            (k_hbm, kv.at[span, 0:rows, 0:half]),
            (v_hbm, kv.at[span, 0:rows, half:2 * half]),
            (seg_hbm, seg_ref),
            (g_hbm, g_ref),
            (q_hbm, q_ref),
        ])
    ]
    for load in loads:
        load.start()

    barrier = pltpu.get_barrier_semaphore()
    for step in range(1, n_shard):
        pl.semaphore_signal(
            barrier, inc=1, device_id=(rep, lax.rem(me + step, n_shard)), device_id_type=MESH
        )
    for step in range(1, n_rep):
        for side in range(2):
            pl.semaphore_signal(
                barrier, inc=1, device_id=(rep_at(step), chip * 2 + side), device_id_type=MESH
            )
    for place in range(span):
        @pl.when(me - span + place < 0)
        def _(place=place):
            kv[place] = jnp.zeros(kv.shape[1:], BF16)
    kv[span, rows:rows + 16, :] = jnp.zeros((16, 2 * half), BF16)
    for load in loads[:3]:
        load.wait()
    seg_row = seg_ref[...].astype(F32)
    kv[span, rows:rows + 16, 0:rows] = jnp.broadcast_to(seg_row, (16, rows)).astype(BF16)
    pl.semaphore_wait(barrier, (n_shard - 1) + 2 * (n_rep - 1))

    def along(d):
        return remote(
            kv.at[span], kv.at[span - 2 * d], zk_send.at[d - 1], zk_recv.at[d - 1],
            rep, me + 2 * d,
        )

    for d in range(1, reach + 1):
        @pl.when(chip + d < n_chip)
        def _(d=d):
            along(d).start()

    def across(d):
        place = span + 1 - 2 * d
        return remote(
            kv.at[place + 1 - 2 * core], kv.at[place], sb_send.at[d - 1], sb_recv.at[d - 1],
            rep, sib,
        )

    def across_exists(d):
        return sib - 2 * d + 1 >= 0

    @pl.when(core == 0)
    def _():
        across(1).start()

    loads[3].wait()

    gt_out[...] = g_ref[...].astype(F32).T.astype(BF16)

    def lanes_of(index):
        return gt.at[:, pl.ds(pl.multiple_of(index * rows, 128), rows)]

    def g_copy(step):
        to = sib if step == 0 else me
        return remote(
            gt_out, lanes_of(slot), g_send.at[step], g_recv.at[slot], rep_at(step), to
        )

    def g_hand(step):
        index = rep_at(n_rep - step) * 2 + core
        return remote(
            lanes_of(index), lanes_of(index), f_send.at[step], g_recv.at[index], rep, sib
        )

    def g_arrived(index):
        remote(gt_out, lanes_of(index), g_send.at[0], g_recv.at[index], rep, sib).wait_recv()

    def g_rest():
        g_arrived(sib_slot)
        for step in range(1, n_rep):
            g_arrived(rep_at(n_rep - step) * 2 + other)

    for step in list(range(1, n_rep)) + [0]:
        g_copy(step).start()
    gt[:, pl.ds(pl.multiple_of(slot * rows, 128), rows)] = gt_out[...]

    for d in range(1, reach + 1):
        @pl.when(chip >= d)
        def _(d=d):
            along(d).wait_recv()
        if d <= reach:
            @pl.when((core == 1) & across_exists(d))
            def _(d=d):
                across(d).start()
        if d + 1 <= reach:
            @pl.when((core == 0) & across_exists(d + 1))
            def _(d=d):
                across(d + 1).start()
    for d in range(1, reach + 1):
        @pl.when(me - 2 * d + 1 >= 0)
        def _(d=d):
            across(d).wait_recv()

    q_seg = jnp.broadcast_to(seg_row, (rows, rows)).T
    for place in range(span + 1):
        k_seg = kv[place, rows:rows + 16, 0:rows].astype(F32)[0:1]
        allowed = q_seg == k_seg
        if place == span:
            q_at = lax.broadcasted_iota(jnp.int32, (rows, rows), 0)
            k_at = lax.broadcasted_iota(jnp.int32, (rows, rows), 1)
            allowed = allowed & (k_at <= q_at)
        else:
            block = lax.broadcasted_iota(jnp.int32, (rows, rows), 0) * 0 + (me - span + place)
            allowed = allowed & (block >= 0)
        bias[:, place * rows:(place + 1) * rows] = jnp.where(allowed, 0.0, -1e30)
        for head in range(KVH):
            lo = head * HD
            span_rows = slice(place * rows, (place + 1) * rows)
            kext[head, span_rows, :] = kv[place, 0:rows, lo:lo + HD]
            vext[head, span_rows, 0:HD] = kv[place, 0:rows, KVH * HD + lo:KVH * HD + lo + HD]
            vext[head, span_rows, HD:2 * HD] = jnp.ones((rows, HD), BF16)

    loads[4].wait()

    targets = [(step, side) for step in range(1, n_rep) for side in range(2)]
    targets = targets + [(0, other), (0, core)]

    def head_of(index, half):
        step, side = targets[index]
        return rep_at(step) * heads_each + side * halves + half

    def a_copy(index, half):
        step, side = targets[index]
        lanes = pl.ds(pl.multiple_of(head_of(index, half) * HD, 128), HD)
        return remote(
            attn_vm.at[:, lanes], a_all.at[half, pl.ds(slot * rows, rows), :],
            a_send.at[half * slots + index], a_recv.at[half * slots + slot],
            rep_at(step), chip * 2 + side,
        )

    def a_arrived(source, half):
        remote(
            attn_vm.at[:, 0:HD], a_all.at[half, pl.ds(source * rows, rows), :],
            a_send.at[0], a_recv.at[half * slots + source], rep, sib,
        ).wait_recv()

    def attend(index, half):
        head = head_of(index, half)
        group = head // (HEADS // KVH)
        lanes = pl.ds(pl.multiple_of(head * HD, 128), HD)
        s = lax.dot_general(
            q_ref[:, lanes], kext[group], (((1,), (1,)), ((), ())),
            preferred_element_type=F32,
        ) + bias[...]
        top = jnp.max(s, axis=-1, keepdims=True)
        p = jnp.exp2((s - top) * SCALE).astype(BF16)
        o = jnp.dot(p, vext[group], preferred_element_type=F32)
        mixed = (o[:, 0:HD] / o[:, HD:2 * HD]).astype(BF16)
        attn_vm[:, lanes] = mixed
        if index == slots - 1:
            a_all[half, pl.ds(slot * rows, rows), :] = mixed
        else:
            a_copy(index, half).start()

    def p_copy(step, half):
        to = lax.rem(me + step, n_shard)
        return remote(
            p_out.at[half, pl.ds(pl.multiple_of(to * out_rows, 16), out_rows), :],
            z_in.at[half, me], p_send.at[half * n_shard + step],
            p_recv.at[half * n_shard + me], rep, to,
        )

    def p_arrived(source, half):
        remote(
            p_out.at[half, 0:out_rows, :], z_in.at[half, source], p_send.at[0],
            p_recv.at[half * n_shard + source], rep, sib,
        ).wait_recv()

    def term(half):
        for step in range(1, n_rep):
            for side in range(2):
                a_arrived(rep_at(n_rep - step) * 2 + side, half)
        a_arrived(sib_slot, half)
        p_out[half] = jnp.dot(gt[...], a_all[half], preferred_element_type=F32).astype(BF16)
        for step in range(1, n_shard):
            p_copy(step, half).start()
        z_in[half, me] = p_out[half, pl.ds(pl.multiple_of(me * out_rows, 16), out_rows), :]

    def o_copy(step, half):
        return remote(
            o_all.at[half, rep], o_all.at[half, rep], o_send.at[half * n_rep + step],
            o_recv.at[half * n_rep + rep], rep_at(step), me,
        )

    def share(half):
        for step in range(1, n_shard):
            p_arrived(lax.rem(me + step, n_shard), half)
        for side in range(2):
            total = z_in[half, side].astype(F32)
            for source in range(1, n_chip):
                total = total + z_in[half, 2 * source + side].astype(F32)
            o_all[half, rep, :, side * HD:(side + 1) * HD] = total.astype(BF16)
        for step in range(1, n_rep):
            o_copy(step, half).start()

    def finish(half):
        for step in range(1, n_rep):
            source = rep_at(step)
            remote(
                o_all.at[half, source], o_all.at[half, source], o_send.at[0],
                o_recv.at[half * n_rep + source], rep, sib,
            ).wait_recv()
        for source in range(n_rep):
            for side in range(2):
                at = (source * heads_each + side * halves + half) * HD
                gw_ref[:, at:at + HD] = o_all[
                    half, source, :, side * HD:(side + 1) * HD
                ].astype(F32)

    for half in range(halves):
        for index in range(slots):
            attend(index, half)
            if half == 0 and index >= slots - n_rep + 1:
                step = index - (slots - n_rep)
                g_arrived(rep_at(n_rep - step) * 2 + core)
                g_hand(step).start()
            if half > 0 and index == EARLY:
                if half == 1:
                    g_rest()
                term(half - 1)
    if halves == 1:
        g_rest()
    term(halves - 1)
    out_copy = pltpu.make_async_copy(attn_vm, attn_hbm, out_sem)
    out_copy.start()
    for half in range(halves):
        share(half)
    for half in range(halves):
        finish(half)

    out_copy.wait()
    for d in range(1, reach + 1):
        @pl.when(chip + d < n_chip)
        def _(d=d):
            along(d).wait_send()

        @pl.when(across_exists(d))
        def _(d=d):
            across(d).wait_send()
    for step in range(n_rep):
        g_copy(step).wait_send()
        if step > 0:
            g_hand(step).wait_send()
    for half in range(halves):
        for index in range(slots - 1):
            a_copy(index, half).wait_send()
        for step in range(1, n_shard):
            p_copy(step, half).wait_send()
        for step in range(1, n_rep):
            o_copy(step, half).wait_send()


def local_narrow(queries, keys, values, segments, grad_output):
    n_rep, n_shard = lax.axis_size("rep"), lax.axis_size("shard")
    rows = queries.shape[1]
    span = MOST // rows
    reach = span // 2
    n_chip = n_shard // 2
    features = grad_output.shape[2]
    out_rows = features // n_shard
    width = HEADS * HD // n_rep
    vmem = pl.BlockSpec(memory_space=pltpu.VMEM)
    dma = pltpu.SemaphoreType.DMA
    attn, grad_weight = pl.pallas_call(
        functools.partial(kernel_narrow, n_rep, n_shard),
        out_shape=(
            jax.ShapeDtypeStruct((rows, HEADS * HD), BF16),
            jax.ShapeDtypeStruct((out_rows, HEADS * HD), F32),
        ),
        in_specs=[pl.BlockSpec(memory_space=pltpu.HBM)] * 5,
        out_specs=(vmem, vmem),
        scratch_shapes=[
            pltpu.VMEM((rows, HEADS * HD), BF16),
            pltpu.VMEM((1, rows), jnp.int32),
            pltpu.VMEM((rows, features), BF16),
            dma((5,)),
            pltpu.VMEM((span + 1, rows + 16, 2 * KVH * HD), BF16),
            pltpu.VMEM((KVH, (span + 1) * rows, HD), BF16),
            pltpu.VMEM((KVH, (span + 1) * rows, 2 * HD), BF16),
            pltpu.VMEM((rows, (span + 1) * rows), F32),
            pltpu.VMEM((2, features // 2, rows), BF16),
            pltpu.VMEM((features // 2, 2 * n_rep * rows), BF16),
            pltpu.VMEM((2 * n_rep * rows, width), BF16),
            pltpu.VMEM((n_chip, out_rows, width), BF16),
            pltpu.VMEM((n_chip, out_rows, width), BF16),
            pltpu.VMEM((n_rep, out_rows, width), BF16),
            dma((reach,)), dma((reach,)), dma((reach,)), dma((reach,)),
            dma((2 * n_rep,)), dma((2 * n_rep,)), dma((2 * n_rep,)), dma((2 * n_rep,)),
            dma((n_chip,)), dma((n_chip,)), dma((n_rep,)), dma((n_rep,)),
        ],
        compiler_params=pltpu.CompilerParams(
            collective_id=0, has_side_effects=True, vmem_limit_bytes=63 * 1024 * 1024
        ),
    )(queries[0], keys[0], values[0], segments, grad_output[0])
    return attn[None], grad_weight


def local_wide(queries, keys, values, segments, grad_output):
    n_rep, n_shard = lax.axis_size("rep"), lax.axis_size("shard")
    rows = queries.shape[1]
    span = MOST // rows
    reach = span // 2
    features = grad_output.shape[2]
    out_rows = features // n_shard
    slots = 2 * n_rep
    halves = HEADS // slots
    vmem = pl.BlockSpec(memory_space=pltpu.VMEM)
    dma = pltpu.SemaphoreType.DMA
    attn, grad_weight = pl.pallas_call(
        functools.partial(kernel, n_rep, n_shard),
        out_shape=(
            jax.ShapeDtypeStruct((rows, HEADS * HD), BF16),
            jax.ShapeDtypeStruct((out_rows, HEADS * HD), F32),
        ),
        in_specs=[pl.BlockSpec(memory_space=pltpu.HBM)] * 5,
        out_specs=(pl.BlockSpec(memory_space=pltpu.HBM), vmem),
        scratch_shapes=[
            pltpu.VMEM((rows, HEADS * HD), BF16),
            pltpu.VMEM((1, rows), jnp.int32),
            pltpu.VMEM((rows, features), BF16),
            dma((5,)),
            pltpu.VMEM((span + 1, rows + 16, 2 * KVH * HD), BF16),
            pltpu.VMEM((KVH, (span + 1) * rows, HD), BF16),
            pltpu.VMEM((KVH, (span + 1) * rows, 2 * HD), BF16),
            pltpu.VMEM((rows, (span + 1) * rows), F32),
            pltpu.VMEM((features, rows), BF16),
            pltpu.VMEM((features, slots * rows), BF16),
            pltpu.VMEM((rows, HEADS * HD), BF16),
            pltpu.VMEM((halves, slots * rows, HD), BF16),
            pltpu.VMEM((halves, features, HD), BF16),
            pltpu.VMEM((halves, n_shard, out_rows, HD), BF16),
            pltpu.VMEM((halves, n_rep, out_rows, 2 * HD), BF16),
            dma((reach,)), dma((reach,)), dma((reach,)), dma((reach,)),
            dma((n_rep,)), dma((slots,)), dma((halves * slots,)), dma((halves * slots,)),
            dma((halves * n_shard,)), dma((halves * n_shard,)),
            dma((halves * n_rep,)), dma((halves * n_rep,)), dma((n_rep,)), dma(()),
        ],
        compiler_params=pltpu.CompilerParams(
            collective_id=1, has_side_effects=True, vmem_limit_bytes=63 * 1024 * 1024
        ),
    )(queries[0], keys[0], values[0], segments, grad_output[0])
    return attn[None], grad_weight


def local(*blocks):
    if HEADS % (2 * lax.axis_size("rep")) == 0:
        return local_wide(*blocks)
    return local_narrow(*blocks)


def solution(mesh):
    placed = (
        P("rep", "shard", None),
        P("rep", "shard", None),
        P("rep", "shard", None),
        P("rep", "shard"),
        P("rep", "shard", None),
    )
    return jax.shard_map(
        local,
        mesh=mesh,
        in_specs=placed,
        out_specs=(P("rep", "shard", None), P("shard", None)),
        check_vma=False,
    )
```

```python
import functools

import jax
import jax.numpy as jnp
from jax import lax
from jax.experimental import pallas as pl
from jax.experimental.pallas import tpu as pltpu
from jax.sharding import PartitionSpec as P

HEADS = 16
KVH = 2
HD = 128
MOST = 512
MESH = pl.DeviceIdType.MESH
EARLY = 4
F32 = jnp.float32
BF16 = jnp.bfloat16
SCALE = HD ** (-0.5) * 1.4426950408889634


def kernel_narrow(
    n_rep, n_shard,
    q_hbm, k_hbm, v_hbm, seg_hbm, g_hbm,
    attn_ref, gw_ref,
    q_ref, seg_ref, g_ref, in_sem, kv, kext, vext, bias, gt_out, gt, a_all, p_out, z_in, o_all,
    zk_send, zk_recv, sb_send, sb_recv, g_send, g_recv, a_send, a_recv,
    p_send, p_recv, o_send, o_recv,
):
    rows = q_ref.shape[0]
    half = KVH * HD
    span = MOST // rows
    reach = span // 2
    n_chip = n_shard // 2
    out_rows = g_ref.shape[1] // n_shard
    heads_each = HEADS // n_rep
    width = heads_each * HD
    rep = lax.axis_index("rep")
    me = lax.axis_index("shard")
    core = lax.rem(me, 2)
    chip = me // 2
    sib = me + 1 - 2 * core
    other = 1 - core
    slot = rep * 2 + core
    sib_slot = rep * 2 + other

    def remote(src, dst, send_sem, recv_sem, to_rep, to_shard):
        return pltpu.make_async_remote_copy(
            src_ref=src, dst_ref=dst, send_sem=send_sem, recv_sem=recv_sem,
            device_id=(to_rep, to_shard), device_id_type=MESH,
        )

    def rep_at(step):
        return lax.rem(rep + step, n_rep)

    def chip_at(step):
        return lax.rem(chip + step, n_chip)

    loads = [
        pltpu.make_async_copy(src, dst, in_sem.at[i])
        for i, (src, dst) in enumerate([
            (k_hbm, kv.at[span, 0:rows, 0:half]),
            (v_hbm, kv.at[span, 0:rows, half:2 * half]),
            (seg_hbm, seg_ref),
            (g_hbm, g_ref),
            (q_hbm, q_ref),
        ])
    ]
    for load in loads:
        load.start()

    barrier = pltpu.get_barrier_semaphore()
    pl.semaphore_signal(barrier, inc=1, device_id=(rep, sib), device_id_type=MESH)
    for step in range(1, n_chip):
        pl.semaphore_signal(
            barrier, inc=1, device_id=(rep, chip_at(step) * 2 + core), device_id_type=MESH
        )
    for step in range(1, n_rep):
        for side in range(2):
            pl.semaphore_signal(
                barrier, inc=1, device_id=(rep_at(step), chip * 2 + side), device_id_type=MESH
            )
    for place in range(span):
        @pl.when(me - span + place < 0)
        def _(place=place):
            kv[place] = jnp.zeros(kv.shape[1:], BF16)
    kv[span, rows:rows + 16, :] = jnp.zeros((16, 2 * half), BF16)
    for load in loads[:3]:
        load.wait()
    seg_row = seg_ref[...].astype(F32)
    kv[span, rows:rows + 16, 0:rows] = jnp.broadcast_to(seg_row, (16, rows)).astype(BF16)
    pl.semaphore_wait(barrier, 1 + (n_chip - 1) + 2 * (n_rep - 1))

    def along(d):
        return remote(
            kv.at[span], kv.at[span - 2 * d], zk_send.at[d - 1], zk_recv.at[d - 1],
            rep, me + 2 * d,
        )

    for d in range(1, reach + 1):
        @pl.when(chip + d < n_chip)
        def _(d=d):
            along(d).start()

    def across(d):
        place = span + 1 - 2 * d
        return remote(
            kv.at[place + 1 - 2 * core], kv.at[place], sb_send.at[d - 1], sb_recv.at[d - 1],
            rep, sib,
        )

    def across_exists(d):
        return sib - 2 * d + 1 >= 0

    @pl.when(core == 0)
    def _():
        across(1).start()

    loads[3].wait()

    for b in range(n_shard):
        if (b * out_rows) % 128 == 0:
            take = max(out_rows, 128)
            piece = g_ref[:, b * out_rows:b * out_rows + take].astype(F32).T.astype(BF16)
        lead = (b * out_rows) % 128 if out_rows < 128 else 0
        gt_out[b % 2, (b // 2) * out_rows:(b // 2 + 1) * out_rows, :] = piece[lead:lead + out_rows]

    def g_copy(step, side):
        return remote(
            gt_out.at[side], gt.at[:, pl.ds(pl.multiple_of(slot * rows, 128), rows)],
            g_send.at[2 * step + side], g_recv.at[slot], rep_at(step), chip * 2 + side,
        )

    for step in range(1, n_rep):
        for side in range(2):
            g_copy(step, side).start()
    g_sib = remote(
        gt_out.at[other], gt.at[:, pl.ds(pl.multiple_of(slot * rows, 128), rows)],
        g_send.at[0], g_recv.at[slot], rep, sib,
    )
    g_sib.start()
    gt[:, pl.ds(pl.multiple_of(slot * rows, 128), rows)] = gt_out[core]

    for d in range(1, reach + 1):
        @pl.when(chip >= d)
        def _(d=d):
            along(d).wait_recv()
        if d <= reach:
            @pl.when((core == 1) & across_exists(d))
            def _(d=d):
                across(d).start()
        if d + 1 <= reach:
            @pl.when((core == 0) & across_exists(d + 1))
            def _(d=d):
                across(d + 1).start()
    for d in range(1, reach + 1):
        @pl.when(me - 2 * d + 1 >= 0)
        def _(d=d):
            across(d).wait_recv()

    q_seg = jnp.broadcast_to(seg_row, (rows, rows)).T
    for place in range(span + 1):
        k_seg = kv[place, rows:rows + 16, 0:rows].astype(F32)[0:1]
        allowed = q_seg == k_seg
        if place == span:
            q_at = lax.broadcasted_iota(jnp.int32, (rows, rows), 0)
            k_at = lax.broadcasted_iota(jnp.int32, (rows, rows), 1)
            allowed = allowed & (k_at <= q_at)
        else:
            block = lax.broadcasted_iota(jnp.int32, (rows, rows), 0) * 0 + (me - span + place)
            allowed = allowed & (block >= 0)
        bias[:, place * rows:(place + 1) * rows] = jnp.where(allowed, 0.0, -1e30)
        for head in range(KVH):
            lo = head * HD
            span_rows = slice(place * rows, (place + 1) * rows)
            kext[head, span_rows, :] = kv[place, 0:rows, lo:lo + HD]
            vext[head, span_rows, 0:HD] = kv[place, 0:rows, KVH * HD + lo:KVH * HD + lo + HD]
            vext[head, span_rows, HD:2 * HD] = jnp.ones((rows, HD), BF16)

    loads[4].wait()

    def columns(step):
        return pl.ds(pl.multiple_of(rep_at(step) * width, 128), width)

    def a_copy(step, side):
        return remote(
            attn_ref.at[:, columns(step)], a_all.at[pl.ds(slot * rows, rows), :],
            a_send.at[2 * step + side], a_recv.at[slot], rep_at(step), chip * 2 + side,
        )

    a_sib = remote(
        attn_ref.at[:, columns(0)], a_all.at[pl.ds(slot * rows, rows), :],
        a_send.at[0], a_recv.at[slot], rep, sib,
    )
    for step in list(range(1, n_rep)) + [0]:
        for j in range(heads_each):
            head = rep_at(step) * heads_each + j
            group = head // (HEADS // KVH)
            lanes = pl.ds(pl.multiple_of(head * HD, 128), HD)
            s = lax.dot_general(
                q_ref[:, lanes], kext[group], (((1,), (1,)), ((), ())),
                preferred_element_type=F32,
            ) + bias[...]
            top = jnp.max(s, axis=-1, keepdims=True)
            p = jnp.exp2((s - top) * SCALE).astype(BF16)
            o = jnp.dot(p, vext[group], preferred_element_type=F32)
            mixed = (o[:, 0:HD] / o[:, HD:2 * HD]).astype(BF16)
            attn_ref[:, lanes] = mixed
            if step == 0:
                a_all[pl.ds(slot * rows, rows), j * HD:(j + 1) * HD] = mixed
        if step == 0:
            a_sib.start()
        else:
            for side in range(2):
                a_copy(step, side).start()

    def arrived(index):
        remote(
            gt_out.at[0], gt.at[:, pl.ds(pl.multiple_of(index * rows, 128), rows)],
            g_send.at[0], g_recv.at[index], rep, sib,
        ).wait_recv()
        remote(
            attn_ref.at[:, columns(0)], a_all.at[pl.ds(index * rows, rows), :],
            a_send.at[0], a_recv.at[index], rep, sib,
        ).wait_recv()

    arrived(sib_slot)
    for step in range(1, n_rep):
        for side in range(2):
            arrived(rep_at(n_rep - step) * 2 + side)

    def term(target):
        block = gt[pl.ds(pl.multiple_of(target * out_rows, 16), out_rows), :]
        return jnp.dot(block, a_all[...], preferred_element_type=F32)

    def p_copy(step):
        return remote(
            p_out.at[chip_at(step)], z_in.at[chip], p_send.at[step], p_recv.at[chip],
            rep, chip_at(step) * 2 + core,
        )

    for step in range(1, n_chip):
        p_out[chip_at(step)] = term(chip_at(step)).astype(BF16)
        p_copy(step).start()
    total = term(chip)
    for step in range(1, n_chip):
        source = chip_at(n_chip - step)
        remote(
            p_out.at[0], z_in.at[source], p_send.at[0], p_recv.at[source], rep, sib
        ).wait_recv()
        total = total + z_in[source].astype(F32)

    o_all[rep] = total.astype(BF16)

    def o_copy(step):
        return remote(
            o_all.at[rep], o_all.at[rep], o_send.at[step], o_recv.at[rep], rep_at(step), me
        )

    for step in range(1, n_rep):
        o_copy(step).start()
    gw_ref[:, columns(0)] = o_all[rep].astype(F32)
    for step in range(1, n_rep):
        source = rep_at(n_rep - step)
        remote(
            o_all.at[source], o_all.at[source], o_send.at[0], o_recv.at[source], rep, sib
        ).wait_recv()
        gw_ref[:, columns(n_rep - step)] = o_all[source].astype(F32)

    for d in range(1, reach + 1):
        @pl.when(chip + d < n_chip)
        def _(d=d):
            along(d).wait_send()

        @pl.when(across_exists(d))
        def _(d=d):
            across(d).wait_send()
    g_sib.wait_send()
    a_sib.wait_send()
    for step in range(1, n_rep):
        for side in range(2):
            g_copy(step, side).wait_send()
            a_copy(step, side).wait_send()
        o_copy(step).wait_send()
    for step in range(1, n_chip):
        p_copy(step).wait_send()


def kernel(
    n_rep, n_shard,
    q_hbm, k_hbm, v_hbm, seg_hbm, g_hbm,
    attn_hbm, gw_ref,
    q_ref, seg_ref, g_ref, in_sem, kv, kext, vext, bias, gt_out, gt, attn_vm, a_all, p_out, z_in, o_all,
    zk_send, zk_recv, sb_send, sb_recv, g_send, g_recv, a_send, a_recv,
    p_send, p_recv, o_send, o_recv, f_send, out_sem,
):
    rows = q_ref.shape[0]
    half = KVH * HD
    span = MOST // rows
    reach = span // 2
    n_chip = n_shard // 2
    out_rows = g_ref.shape[1] // n_shard
    heads_each = HEADS // n_rep
    halves = heads_each // 2
    slots = 2 * n_rep
    rep = lax.axis_index("rep")
    me = lax.axis_index("shard")
    core = lax.rem(me, 2)
    chip = me // 2
    sib = me + 1 - 2 * core
    other = 1 - core
    slot = rep * 2 + core
    sib_slot = rep * 2 + other

    def remote(src, dst, send_sem, recv_sem, to_rep, to_shard):
        return pltpu.make_async_remote_copy(
            src_ref=src, dst_ref=dst, send_sem=send_sem, recv_sem=recv_sem,
            device_id=(to_rep, to_shard), device_id_type=MESH,
        )

    def rep_at(step):
        return lax.rem(rep + step, n_rep)

    loads = [
        pltpu.make_async_copy(src, dst, in_sem.at[i])
        for i, (src, dst) in enumerate([
            (k_hbm, kv.at[span, 0:rows, 0:half]),
            (v_hbm, kv.at[span, 0:rows, half:2 * half]),
            (seg_hbm, seg_ref),
            (g_hbm, g_ref),
            (q_hbm, q_ref),
        ])
    ]
    for load in loads:
        load.start()

    barrier = pltpu.get_barrier_semaphore()
    for step in range(1, n_shard):
        pl.semaphore_signal(
            barrier, inc=1, device_id=(rep, lax.rem(me + step, n_shard)), device_id_type=MESH
        )
    for step in range(1, n_rep):
        for side in range(2):
            pl.semaphore_signal(
                barrier, inc=1, device_id=(rep_at(step), chip * 2 + side), device_id_type=MESH
            )
    for place in range(span):
        @pl.when(me - span + place < 0)
        def _(place=place):
            kv[place] = jnp.zeros(kv.shape[1:], BF16)
    kv[span, rows:rows + 16, :] = jnp.zeros((16, 2 * half), BF16)
    for load in loads[:3]:
        load.wait()
    seg_row = seg_ref[...].astype(F32)
    kv[span, rows:rows + 16, 0:rows] = jnp.broadcast_to(seg_row, (16, rows)).astype(BF16)
    pl.semaphore_wait(barrier, (n_shard - 1) + 2 * (n_rep - 1))

    def along(d):
        return remote(
            kv.at[span], kv.at[span - 2 * d], zk_send.at[d - 1], zk_recv.at[d - 1],
            rep, me + 2 * d,
        )

    for d in range(1, reach + 1):
        @pl.when(chip + d < n_chip)
        def _(d=d):
            along(d).start()

    def across(d):
        place = span + 1 - 2 * d
        return remote(
            kv.at[place + 1 - 2 * core], kv.at[place], sb_send.at[d - 1], sb_recv.at[d - 1],
            rep, sib,
        )

    def across_exists(d):
        return sib - 2 * d + 1 >= 0

    @pl.when(core == 0)
    def _():
        across(1).start()

    loads[3].wait()

    gt_out[...] = g_ref[...].astype(F32).T.astype(BF16)

    part = gt.shape[0] // 2

    def lanes_of(index, piece):
        return gt.at[
            piece * part:(piece + 1) * part, pl.ds(pl.multiple_of(index * rows, 128), rows)
        ]

    def plane(axis):
        bit = rep % 2 if axis != 1 else rep // 2
        first = 1 - 2 * bit if axis == 0 else 2 - 4 * bit
        if axis == 2:
            first = 3 - 2 * rep
        return rep + first

    def g_copy(axis, piece):
        to_rep, to = (rep, sib) if axis == 2 else (plane(axis), me)
        return remote(
            gt_out.at[piece * part:(piece + 1) * part], lanes_of(slot, piece),
            g_send.at[2 * axis + piece], g_recv.at[2 * slot + piece], to_rep, to,
        )

    def g_corner(piece):
        index = plane(piece) * 2 + core
        return remote(
            lanes_of(index, piece), lanes_of(index, piece), g_send.at[6 + piece],
            g_recv.at[2 * index + piece], plane(1 - piece), me,
        )

    def g_hand(axis, piece):
        index = plane(axis) * 2 + core
        return remote(
            lanes_of(index, piece), lanes_of(index, piece), f_send.at[2 * axis + piece],
            g_recv.at[2 * index + piece], rep, sib,
        )

    def g_arrived(index, piece):
        remote(
            gt_out.at[0:part], lanes_of(index, piece), g_send.at[0],
            g_recv.at[2 * index + piece], rep, sib,
        ).wait_recv()

    def g_rest():
        for piece in range(2):
            g_arrived(sib_slot, piece)
            for axis in range(3):
                g_arrived(plane(axis) * 2 + other, piece)

    for axis, piece in [(0, 0), (1, 1), (0, 1), (1, 0), (2, 0), (2, 1)]:
        g_copy(axis, piece).start()
    gt[:, pl.ds(pl.multiple_of(slot * rows, 128), rows)] = gt_out[...]

    for d in range(1, reach + 1):
        @pl.when(chip >= d)
        def _(d=d):
            along(d).wait_recv()
        if d <= reach:
            @pl.when((core == 1) & across_exists(d))
            def _(d=d):
                across(d).start()
        if d + 1 <= reach:
            @pl.when((core == 0) & across_exists(d + 1))
            def _(d=d):
                across(d + 1).start()
    for d in range(1, reach + 1):
        @pl.when(me - 2 * d + 1 >= 0)
        def _(d=d):
            across(d).wait_recv()

    for piece in range(2):
        g_arrived(plane(piece) * 2 + core, piece)
        g_corner(piece).start()
        g_hand(piece, piece).start()

    q_seg = jnp.broadcast_to(seg_row, (rows, rows)).T
    for place in range(span + 1):
        k_seg = kv[place, rows:rows + 16, 0:rows].astype(F32)[0:1]
        allowed = q_seg == k_seg
        if place == span:
            q_at = lax.broadcasted_iota(jnp.int32, (rows, rows), 0)
            k_at = lax.broadcasted_iota(jnp.int32, (rows, rows), 1)
            allowed = allowed & (k_at <= q_at)
        else:
            block = lax.broadcasted_iota(jnp.int32, (rows, rows), 0) * 0 + (me - span + place)
            allowed = allowed & (block >= 0)
        bias[:, place * rows:(place + 1) * rows] = jnp.where(allowed, 0.0, -1e30)
        for head in range(KVH):
            lo = head * HD
            span_rows = slice(place * rows, (place + 1) * rows)
            kext[head, span_rows, :] = kv[place, 0:rows, lo:lo + HD]
            vext[head, span_rows, 0:HD] = kv[place, 0:rows, KVH * HD + lo:KVH * HD + lo + HD]
            vext[head, span_rows, HD:2 * HD] = jnp.ones((rows, HD), BF16)

    loads[4].wait()

    targets = [(step, side) for step in range(1, n_rep) for side in range(2)]
    targets = targets + [(0, other), (0, core)]

    def head_of(index, half):
        step, side = targets[index]
        return rep_at(step) * heads_each + side * halves + half

    def a_copy(index, half):
        step, side = targets[index]
        lanes = pl.ds(pl.multiple_of(head_of(index, half) * HD, 128), HD)
        return remote(
            attn_vm.at[:, lanes], a_all.at[half, pl.ds(slot * rows, rows), :],
            a_send.at[half * slots + index], a_recv.at[half * slots + slot],
            rep_at(step), chip * 2 + side,
        )

    def a_arrived(source, half):
        remote(
            attn_vm.at[:, 0:HD], a_all.at[half, pl.ds(source * rows, rows), :],
            a_send.at[0], a_recv.at[half * slots + source], rep, sib,
        ).wait_recv()

    def attend(index, half):
        head = head_of(index, half)
        group = head // (HEADS // KVH)
        lanes = pl.ds(pl.multiple_of(head * HD, 128), HD)
        s = lax.dot_general(
            q_ref[:, lanes], kext[group], (((1,), (1,)), ((), ())),
            preferred_element_type=F32,
        ) + bias[...]
        top = jnp.max(s, axis=-1, keepdims=True)
        p = jnp.exp2((s - top) * SCALE).astype(BF16)
        o = jnp.dot(p, vext[group], preferred_element_type=F32)
        mixed = (o[:, 0:HD] / o[:, HD:2 * HD]).astype(BF16)
        attn_vm[:, lanes] = mixed
        if index == slots - 1:
            a_all[half, pl.ds(slot * rows, rows), :] = mixed
        else:
            a_copy(index, half).start()

    def p_copy(step, half):
        to = lax.rem(me + step, n_shard)
        return remote(
            p_out.at[half, pl.ds(pl.multiple_of(to * out_rows, 16), out_rows), :],
            z_in.at[half, me], p_send.at[half * n_shard + step],
            p_recv.at[half * n_shard + me], rep, to,
        )

    def p_arrived(source, half):
        remote(
            p_out.at[half, 0:out_rows, :], z_in.at[half, source], p_send.at[0],
            p_recv.at[half * n_shard + source], rep, sib,
        ).wait_recv()

    def term(half):
        for step in range(1, n_rep):
            for side in range(2):
                a_arrived(rep_at(n_rep - step) * 2 + side, half)
        a_arrived(sib_slot, half)
        p_out[half] = jnp.dot(gt[...], a_all[half], preferred_element_type=F32).astype(BF16)
        for step in range(1, n_shard):
            p_copy(step, half).start()
        z_in[half, me] = p_out[half, pl.ds(pl.multiple_of(me * out_rows, 16), out_rows), :]

    def o_copy(step, half):
        return remote(
            o_all.at[half, rep], o_all.at[half, rep], o_send.at[half * n_rep + step],
            o_recv.at[half * n_rep + rep], rep_at(step), me,
        )

    def share(half):
        for step in range(1, n_shard):
            p_arrived(lax.rem(me + step, n_shard), half)
        for side in range(2):
            total = z_in[half, side].astype(F32)
            for source in range(1, n_chip):
                total = total + z_in[half, 2 * source + side].astype(F32)
            o_all[half, rep, :, side * HD:(side + 1) * HD] = total.astype(BF16)
        for step in range(1, n_rep):
            o_copy(step, half).start()

    def finish(half):
        for step in range(1, n_rep):
            source = rep_at(step)
            remote(
                o_all.at[half, source], o_all.at[half, source], o_send.at[0],
                o_recv.at[half * n_rep + source], rep, sib,
            ).wait_recv()
        for source in range(n_rep):
            for side in range(2):
                at = (source * heads_each + side * halves + half) * HD
                gw_ref[:, at:at + HD] = o_all[
                    half, source, :, side * HD:(side + 1) * HD
                ].astype(F32)

    for half in range(halves):
        for index in range(slots):
            attend(index, half)
            if half == 0 and index >= slots - 2:
                hands = [(0, 1), (1, 0)] if index == slots - 2 else [(2, 0), (2, 1)]
                for axis, piece in hands:
                    g_arrived(plane(axis) * 2 + core, piece)
                    g_hand(axis, piece).start()
            if half > 0 and index == EARLY:
                if half == 1:
                    g_rest()
                term(half - 1)
    if halves == 1:
        g_rest()
    term(halves - 1)
    out_copy = pltpu.make_async_copy(attn_vm, attn_hbm, out_sem)
    out_copy.start()
    for half in range(halves):
        share(half)
    for half in range(halves):
        finish(half)

    out_copy.wait()
    for d in range(1, reach + 1):
        @pl.when(chip + d < n_chip)
        def _(d=d):
            along(d).wait_send()

        @pl.when(across_exists(d))
        def _(d=d):
            across(d).wait_send()
    for piece in range(2):
        for axis in range(3):
            g_copy(axis, piece).wait_send()
            g_hand(axis, piece).wait_send()
        g_corner(piece).wait_send()
    for half in range(halves):
        for index in range(slots - 1):
            a_copy(index, half).wait_send()
        for step in range(1, n_shard):
            p_copy(step, half).wait_send()
        for step in range(1, n_rep):
            o_copy(step, half).wait_send()


def local_narrow(queries, keys, values, segments, grad_output):
    n_rep, n_shard = lax.axis_size("rep"), lax.axis_size("shard")
    rows = queries.shape[1]
    span = MOST // rows
    reach = span // 2
    n_chip = n_shard // 2
    features = grad_output.shape[2]
    out_rows = features // n_shard
    width = HEADS * HD // n_rep
    vmem = pl.BlockSpec(memory_space=pltpu.VMEM)
    dma = pltpu.SemaphoreType.DMA
    attn, grad_weight = pl.pallas_call(
        functools.partial(kernel_narrow, n_rep, n_shard),
        out_shape=(
            jax.ShapeDtypeStruct((rows, HEADS * HD), BF16),
            jax.ShapeDtypeStruct((out_rows, HEADS * HD), F32),
        ),
        in_specs=[pl.BlockSpec(memory_space=pltpu.HBM)] * 5,
        out_specs=(vmem, vmem),
        scratch_shapes=[
            pltpu.VMEM((rows, HEADS * HD), BF16),
            pltpu.VMEM((1, rows), jnp.int32),
            pltpu.VMEM((rows, features), BF16),
            dma((5,)),
            pltpu.VMEM((span + 1, rows + 16, 2 * KVH * HD), BF16),
            pltpu.VMEM((KVH, (span + 1) * rows, HD), BF16),
            pltpu.VMEM((KVH, (span + 1) * rows, 2 * HD), BF16),
            pltpu.VMEM((rows, (span + 1) * rows), F32),
            pltpu.VMEM((2, features // 2, rows), BF16),
            pltpu.VMEM((features // 2, 2 * n_rep * rows), BF16),
            pltpu.VMEM((2 * n_rep * rows, width), BF16),
            pltpu.VMEM((n_chip, out_rows, width), BF16),
            pltpu.VMEM((n_chip, out_rows, width), BF16),
            pltpu.VMEM((n_rep, out_rows, width), BF16),
            dma((reach,)), dma((reach,)), dma((reach,)), dma((reach,)),
            dma((2 * n_rep,)), dma((2 * n_rep,)), dma((2 * n_rep,)), dma((2 * n_rep,)),
            dma((n_chip,)), dma((n_chip,)), dma((n_rep,)), dma((n_rep,)),
        ],
        compiler_params=pltpu.CompilerParams(
            collective_id=0, has_side_effects=True, vmem_limit_bytes=63 * 1024 * 1024
        ),
    )(queries[0], keys[0], values[0], segments, grad_output[0])
    return attn[None], grad_weight


def local_wide(queries, keys, values, segments, grad_output):
    n_rep, n_shard = lax.axis_size("rep"), lax.axis_size("shard")
    rows = queries.shape[1]
    span = MOST // rows
    reach = span // 2
    features = grad_output.shape[2]
    out_rows = features // n_shard
    slots = 2 * n_rep
    halves = HEADS // slots
    vmem = pl.BlockSpec(memory_space=pltpu.VMEM)
    dma = pltpu.SemaphoreType.DMA
    attn, grad_weight = pl.pallas_call(
        functools.partial(kernel, n_rep, n_shard),
        out_shape=(
            jax.ShapeDtypeStruct((rows, HEADS * HD), BF16),
            jax.ShapeDtypeStruct((out_rows, HEADS * HD), F32),
        ),
        in_specs=[pl.BlockSpec(memory_space=pltpu.HBM)] * 5,
        out_specs=(pl.BlockSpec(memory_space=pltpu.HBM), vmem),
        scratch_shapes=[
            pltpu.VMEM((rows, HEADS * HD), BF16),
            pltpu.VMEM((1, rows), jnp.int32),
            pltpu.VMEM((rows, features), BF16),
            dma((5,)),
            pltpu.VMEM((span + 1, rows + 16, 2 * KVH * HD), BF16),
            pltpu.VMEM((KVH, (span + 1) * rows, HD), BF16),
            pltpu.VMEM((KVH, (span + 1) * rows, 2 * HD), BF16),
            pltpu.VMEM((rows, (span + 1) * rows), F32),
            pltpu.VMEM((features, rows), BF16),
            pltpu.VMEM((features, slots * rows), BF16),
            pltpu.VMEM((rows, HEADS * HD), BF16),
            pltpu.VMEM((halves, slots * rows, HD), BF16),
            pltpu.VMEM((halves, features, HD), BF16),
            pltpu.VMEM((halves, n_shard, out_rows, HD), BF16),
            pltpu.VMEM((halves, n_rep, out_rows, 2 * HD), BF16),
            dma((reach,)), dma((reach,)), dma((reach,)), dma((reach,)),
            dma((8,)), dma((2 * slots,)), dma((halves * slots,)), dma((halves * slots,)),
            dma((halves * n_shard,)), dma((halves * n_shard,)),
            dma((halves * n_rep,)), dma((halves * n_rep,)), dma((6,)), dma(()),
        ],
        compiler_params=pltpu.CompilerParams(
            collective_id=1, has_side_effects=True, vmem_limit_bytes=63 * 1024 * 1024
        ),
    )(queries[0], keys[0], values[0], segments, grad_output[0])
    return attn[None], grad_weight


def local(*blocks):
    if lax.axis_size("rep") == 4:
        return local_wide(*blocks)
    return local_narrow(*blocks)


def solution(mesh):
    placed = (
        P("rep", "shard", None),
        P("rep", "shard", None),
        P("rep", "shard", None),
        P("rep", "shard"),
        P("rep", "shard", None),
    )
    return jax.shard_map(
        local,
        mesh=mesh,
        in_specs=placed,
        out_specs=(P("rep", "shard", None), P("shard", None)),
        check_vma=False,
    )
```

```python
import functools

import jax
import jax.numpy as jnp
from jax import lax
from jax.experimental import pallas as pl
from jax.experimental.pallas import tpu as pltpu
from jax.sharding import PartitionSpec as P

HEADS = 16
KVH = 2
HD = 128
MOST = 512
MESH = pl.DeviceIdType.MESH
EARLY = 4
F32 = jnp.float32
BF16 = jnp.bfloat16
SCALE = HD ** (-0.5) * 1.4426950408889634


def kernel_narrow(
    n_rep, n_shard,
    q_hbm, k_hbm, v_hbm, seg_hbm, g_hbm,
    attn_ref, gw_ref,
    q_ref, seg_ref, g_ref, in_sem, kv, kext, vext, bias, gt_out, gt, a_all, p_out, z_in, o_all,
    zk_send, zk_recv, sb_send, sb_recv, g_send, g_recv, a_send, a_recv,
    p_send, p_recv, o_send, o_recv,
):
    rows = q_ref.shape[0]
    half = KVH * HD
    span = MOST // rows
    reach = span // 2
    n_chip = n_shard // 2
    out_rows = g_ref.shape[1] // n_shard
    heads_each = HEADS // n_rep
    width = heads_each * HD
    rep = lax.axis_index("rep")
    me = lax.axis_index("shard")
    core = lax.rem(me, 2)
    chip = me // 2
    sib = me + 1 - 2 * core
    other = 1 - core
    slot = rep * 2 + core
    sib_slot = rep * 2 + other

    def remote(src, dst, send_sem, recv_sem, to_rep, to_shard):
        return pltpu.make_async_remote_copy(
            src_ref=src, dst_ref=dst, send_sem=send_sem, recv_sem=recv_sem,
            device_id=(to_rep, to_shard), device_id_type=MESH,
        )

    def rep_at(step):
        return lax.rem(rep + step, n_rep)

    def chip_at(step):
        return lax.rem(chip + step, n_chip)

    loads = [
        pltpu.make_async_copy(src, dst, in_sem.at[i])
        for i, (src, dst) in enumerate([
            (k_hbm, kv.at[span, 0:rows, 0:half]),
            (v_hbm, kv.at[span, 0:rows, half:2 * half]),
            (seg_hbm, seg_ref),
            (g_hbm, g_ref),
            (q_hbm, q_ref),
        ])
    ]
    for load in loads:
        load.start()

    barrier = pltpu.get_barrier_semaphore()
    pl.semaphore_signal(barrier, inc=1, device_id=(rep, sib), device_id_type=MESH)
    for step in range(1, n_chip):
        pl.semaphore_signal(
            barrier, inc=1, device_id=(rep, chip_at(step) * 2 + core), device_id_type=MESH
        )
    for step in range(1, n_rep):
        for side in range(2):
            pl.semaphore_signal(
                barrier, inc=1, device_id=(rep_at(step), chip * 2 + side), device_id_type=MESH
            )
    for place in range(span):
        @pl.when(me - span + place < 0)
        def _(place=place):
            kv[place] = jnp.zeros(kv.shape[1:], BF16)
    kv[span, rows:rows + 16, :] = jnp.zeros((16, 2 * half), BF16)
    for load in loads[:3]:
        load.wait()
    seg_row = seg_ref[...].astype(F32)
    kv[span, rows:rows + 16, 0:rows] = jnp.broadcast_to(seg_row, (16, rows)).astype(BF16)
    pl.semaphore_wait(barrier, 1 + (n_chip - 1) + 2 * (n_rep - 1))

    def along(d):
        return remote(
            kv.at[span], kv.at[span - 2 * d], zk_send.at[d - 1], zk_recv.at[d - 1],
            rep, me + 2 * d,
        )

    for d in range(1, reach + 1):
        @pl.when(chip + d < n_chip)
        def _(d=d):
            along(d).start()

    def across(d):
        place = span + 1 - 2 * d
        return remote(
            kv.at[place + 1 - 2 * core], kv.at[place], sb_send.at[d - 1], sb_recv.at[d - 1],
            rep, sib,
        )

    def across_exists(d):
        return sib - 2 * d + 1 >= 0

    @pl.when(core == 0)
    def _():
        across(1).start()

    loads[3].wait()

    for b in range(n_shard):
        if (b * out_rows) % 128 == 0:
            take = max(out_rows, 128)
            piece = g_ref[:, b * out_rows:b * out_rows + take].astype(F32).T.astype(BF16)
        lead = (b * out_rows) % 128 if out_rows < 128 else 0
        gt_out[b % 2, (b // 2) * out_rows:(b // 2 + 1) * out_rows, :] = piece[lead:lead + out_rows]

    def g_copy(step, side):
        return remote(
            gt_out.at[side], gt.at[:, pl.ds(pl.multiple_of(slot * rows, 128), rows)],
            g_send.at[2 * step + side], g_recv.at[slot], rep_at(step), chip * 2 + side,
        )

    for step in range(1, n_rep):
        for side in range(2):
            g_copy(step, side).start()
    g_sib = remote(
        gt_out.at[other], gt.at[:, pl.ds(pl.multiple_of(slot * rows, 128), rows)],
        g_send.at[0], g_recv.at[slot], rep, sib,
    )
    g_sib.start()
    gt[:, pl.ds(pl.multiple_of(slot * rows, 128), rows)] = gt_out[core]

    for d in range(1, reach + 1):
        @pl.when(chip >= d)
        def _(d=d):
            along(d).wait_recv()
        if d <= reach:
            @pl.when((core == 1) & across_exists(d))
            def _(d=d):
                across(d).start()
        if d + 1 <= reach:
            @pl.when((core == 0) & across_exists(d + 1))
            def _(d=d):
                across(d + 1).start()
    for d in range(1, reach + 1):
        @pl.when(me - 2 * d + 1 >= 0)
        def _(d=d):
            across(d).wait_recv()

    q_seg = jnp.broadcast_to(seg_row, (rows, rows)).T
    for place in range(span + 1):
        k_seg = kv[place, rows:rows + 16, 0:rows].astype(F32)[0:1]
        allowed = q_seg == k_seg
        if place == span:
            q_at = lax.broadcasted_iota(jnp.int32, (rows, rows), 0)
            k_at = lax.broadcasted_iota(jnp.int32, (rows, rows), 1)
            allowed = allowed & (k_at <= q_at)
        else:
            block = lax.broadcasted_iota(jnp.int32, (rows, rows), 0) * 0 + (me - span + place)
            allowed = allowed & (block >= 0)
        bias[:, place * rows:(place + 1) * rows] = jnp.where(allowed, 0.0, -1e30)
        for head in range(KVH):
            lo = head * HD
            span_rows = slice(place * rows, (place + 1) * rows)
            kext[head, span_rows, :] = kv[place, 0:rows, lo:lo + HD]
            vext[head, span_rows, 0:HD] = kv[place, 0:rows, KVH * HD + lo:KVH * HD + lo + HD]
            vext[head, span_rows, HD:2 * HD] = jnp.ones((rows, HD), BF16)

    loads[4].wait()

    def columns(step):
        return pl.ds(pl.multiple_of(rep_at(step) * width, 128), width)

    def a_copy(step, side):
        return remote(
            attn_ref.at[:, columns(step)], a_all.at[pl.ds(slot * rows, rows), :],
            a_send.at[2 * step + side], a_recv.at[slot], rep_at(step), chip * 2 + side,
        )

    a_sib = remote(
        attn_ref.at[:, columns(0)], a_all.at[pl.ds(slot * rows, rows), :],
        a_send.at[0], a_recv.at[slot], rep, sib,
    )
    for step in list(range(1, n_rep)) + [0]:
        for j in range(heads_each):
            head = rep_at(step) * heads_each + j
            group = head // (HEADS // KVH)
            lanes = pl.ds(pl.multiple_of(head * HD, 128), HD)
            s = lax.dot_general(
                q_ref[:, lanes], kext[group], (((1,), (1,)), ((), ())),
                preferred_element_type=F32,
            ) + bias[...]
            top = jnp.max(s, axis=-1, keepdims=True)
            p = jnp.exp2((s - top) * SCALE).astype(BF16)
            o = jnp.dot(p, vext[group], preferred_element_type=F32)
            mixed = (o[:, 0:HD] / o[:, HD:2 * HD]).astype(BF16)
            attn_ref[:, lanes] = mixed
            if step == 0:
                a_all[pl.ds(slot * rows, rows), j * HD:(j + 1) * HD] = mixed
        if step == 0:
            a_sib.start()
        else:
            for side in range(2):
                a_copy(step, side).start()

    def arrived(index):
        remote(
            gt_out.at[0], gt.at[:, pl.ds(pl.multiple_of(index * rows, 128), rows)],
            g_send.at[0], g_recv.at[index], rep, sib,
        ).wait_recv()
        remote(
            attn_ref.at[:, columns(0)], a_all.at[pl.ds(index * rows, rows), :],
            a_send.at[0], a_recv.at[index], rep, sib,
        ).wait_recv()

    arrived(sib_slot)
    for step in range(1, n_rep):
        for side in range(2):
            arrived(rep_at(n_rep - step) * 2 + side)

    def term(target):
        block = gt[pl.ds(pl.multiple_of(target * out_rows, 16), out_rows), :]
        return jnp.dot(block, a_all[...], preferred_element_type=F32)

    def p_copy(step):
        return remote(
            p_out.at[chip_at(step)], z_in.at[chip], p_send.at[step], p_recv.at[chip],
            rep, chip_at(step) * 2 + core,
        )

    for step in range(1, n_chip):
        p_out[chip_at(step)] = term(chip_at(step)).astype(BF16)
        p_copy(step).start()
    total = term(chip)
    for step in range(1, n_chip):
        source = chip_at(n_chip - step)
        remote(
            p_out.at[0], z_in.at[source], p_send.at[0], p_recv.at[source], rep, sib
        ).wait_recv()
        total = total + z_in[source].astype(F32)

    o_all[rep] = total.astype(BF16)

    def o_copy(step):
        return remote(
            o_all.at[rep], o_all.at[rep], o_send.at[step], o_recv.at[rep], rep_at(step), me
        )

    for step in range(1, n_rep):
        o_copy(step).start()
    gw_ref[:, columns(0)] = o_all[rep].astype(F32)
    for step in range(1, n_rep):
        source = rep_at(n_rep - step)
        remote(
            o_all.at[source], o_all.at[source], o_send.at[0], o_recv.at[source], rep, sib
        ).wait_recv()
        gw_ref[:, columns(n_rep - step)] = o_all[source].astype(F32)

    for d in range(1, reach + 1):
        @pl.when(chip + d < n_chip)
        def _(d=d):
            along(d).wait_send()

        @pl.when(across_exists(d))
        def _(d=d):
            across(d).wait_send()
    g_sib.wait_send()
    a_sib.wait_send()
    for step in range(1, n_rep):
        for side in range(2):
            g_copy(step, side).wait_send()
            a_copy(step, side).wait_send()
        o_copy(step).wait_send()
    for step in range(1, n_chip):
        p_copy(step).wait_send()


def kernel(
    n_rep, n_shard,
    q_hbm, k_hbm, v_hbm, seg_hbm, g_hbm,
    attn_hbm, gw_ref,
    q_ref, seg_ref, g_ref, in_sem, kv, kext, vext, bias, gt_out, gt, attn_vm, a_all, p_out, z_in, o_all,
    zk_send, zk_recv, sb_send, sb_recv, g_send, g_recv, a_send, a_recv,
    p_send, p_recv, o_send, o_recv, f_send, out_sem,
):
    rows = q_ref.shape[0]
    half = KVH * HD
    span = MOST // rows
    reach = span // 2
    n_chip = n_shard // 2
    out_rows = g_ref.shape[1] // n_shard
    heads_each = HEADS // n_rep
    halves = heads_each // 2
    slots = 2 * n_rep
    rep = lax.axis_index("rep")
    me = lax.axis_index("shard")
    core = lax.rem(me, 2)
    chip = me // 2
    sib = me + 1 - 2 * core
    other = 1 - core
    slot = rep * 2 + core
    sib_slot = rep * 2 + other

    def remote(src, dst, send_sem, recv_sem, to_rep, to_shard):
        return pltpu.make_async_remote_copy(
            src_ref=src, dst_ref=dst, send_sem=send_sem, recv_sem=recv_sem,
            device_id=(to_rep, to_shard), device_id_type=MESH,
        )

    def rep_at(step):
        return lax.rem(rep + step, n_rep)

    loads = [
        pltpu.make_async_copy(src, dst, in_sem.at[i])
        for i, (src, dst) in enumerate([
            (k_hbm, kv.at[span, 0:rows, 0:half]),
            (v_hbm, kv.at[span, 0:rows, half:2 * half]),
            (seg_hbm, seg_ref),
            (g_hbm, g_ref),
            (q_hbm, q_ref),
        ])
    ]
    for load in loads:
        load.start()

    barrier = pltpu.get_barrier_semaphore()
    for step in range(1, n_shard):
        pl.semaphore_signal(
            barrier, inc=1, device_id=(rep, lax.rem(me + step, n_shard)), device_id_type=MESH
        )
    for step in range(1, n_rep):
        for side in range(2):
            pl.semaphore_signal(
                barrier, inc=1, device_id=(rep_at(step), chip * 2 + side), device_id_type=MESH
            )
    for place in range(span):
        @pl.when(me - span + place < 0)
        def _(place=place):
            kv[place] = jnp.zeros(kv.shape[1:], BF16)
    kv[span, rows:rows + 16, :] = jnp.zeros((16, 2 * half), BF16)
    for load in loads[:3]:
        load.wait()
    seg_row = seg_ref[...].astype(F32)
    kv[span, rows:rows + 16, 0:rows] = jnp.broadcast_to(seg_row, (16, rows)).astype(BF16)
    pl.semaphore_wait(barrier, (n_shard - 1) + 2 * (n_rep - 1))

    def along(d):
        return remote(
            kv.at[span], kv.at[span - 2 * d], zk_send.at[d - 1], zk_recv.at[d - 1],
            rep, me + 2 * d,
        )

    for d in range(1, reach + 1):
        @pl.when(chip + d < n_chip)
        def _(d=d):
            along(d).start()

    def across(d):
        place = span + 1 - 2 * d
        return remote(
            kv.at[place + 1 - 2 * core], kv.at[place], sb_send.at[d - 1], sb_recv.at[d - 1],
            rep, sib,
        )

    def across_exists(d):
        return sib - 2 * d + 1 >= 0

    @pl.when(core == 0)
    def _():
        across(1).start()

    loads[3].wait()

    gt_out[...] = g_ref[...].astype(F32).T.astype(BF16)

    def lanes_of(index):
        return gt.at[:, pl.ds(pl.multiple_of(index * rows, 128), rows)]

    def g_copy(step):
        to = sib if step == 0 else me
        return remote(
            gt_out, lanes_of(slot), g_send.at[step], g_recv.at[slot], rep_at(step), to
        )

    def g_hand(step):
        index = rep_at(n_rep - step) * 2 + core
        return remote(
            lanes_of(index), lanes_of(index), f_send.at[step], g_recv.at[index], rep, sib
        )

    def g_arrived(index):
        remote(gt_out, lanes_of(index), g_send.at[0], g_recv.at[index], rep, sib).wait_recv()

    def g_rest():
        g_arrived(sib_slot)
        for step in range(1, n_rep):
            g_arrived(rep_at(n_rep - step) * 2 + other)

    for step in range(1, n_rep):
        g_copy(step).start()
    gt[:, pl.ds(pl.multiple_of(slot * rows, 128), rows)] = gt_out[...]

    q_seg = jnp.broadcast_to(seg_row, (rows, rows)).T

    def prepare(place):
        k_seg = kv[place, rows:rows + 16, 0:rows].astype(F32)[0:1]
        allowed = q_seg == k_seg
        if place == span:
            q_at = lax.broadcasted_iota(jnp.int32, (rows, rows), 0)
            k_at = lax.broadcasted_iota(jnp.int32, (rows, rows), 1)
            allowed = allowed & (k_at <= q_at)
        else:
            block = lax.broadcasted_iota(jnp.int32, (rows, rows), 0) * 0 + (me - span + place)
            allowed = allowed & (block >= 0)
        bias[:, place * rows:(place + 1) * rows] = jnp.where(allowed, 0.0, -1e30)
        for head in range(KVH):
            lo = head * HD
            span_rows = slice(place * rows, (place + 1) * rows)
            kext[head, span_rows, :] = kv[place, 0:rows, lo:lo + HD]
            vext[head, span_rows, 0:HD] = kv[place, 0:rows, KVH * HD + lo:KVH * HD + lo + HD]
            vext[head, span_rows, HD:2 * HD] = jnp.ones((rows, HD), BF16)

    prepare(span)

    for d in range(1, reach + 1):
        @pl.when(chip >= d)
        def _(d=d):
            along(d).wait_recv()
        if d <= reach:
            @pl.when((core == 1) & across_exists(d))
            def _(d=d):
                across(d).start()
        if d + 1 <= reach:
            @pl.when((core == 0) & across_exists(d + 1))
            def _(d=d):
                across(d + 1).start()
    for d in range(1, reach + 1):
        @pl.when(me - 2 * d + 1 >= 0)
        def _(d=d):
            across(d).wait_recv()
    g_copy(0).start()
    for place in range(span):
        prepare(place)
    loads[4].wait()

    targets = [(step, side) for step in range(1, n_rep) for side in range(2)]
    targets = targets + [(0, other), (0, core)]

    def head_of(index, half):
        step, side = targets[index]
        return rep_at(step) * heads_each + side * halves + half

    def a_copy(index, half):
        step, side = targets[index]
        lanes = pl.ds(pl.multiple_of(head_of(index, half) * HD, 128), HD)
        return remote(
            attn_vm.at[:, lanes], a_all.at[half, pl.ds(slot * rows, rows), :],
            a_send.at[half * slots + index], a_recv.at[half * slots + slot],
            rep_at(step), chip * 2 + side,
        )

    def a_arrived(source, half):
        remote(
            attn_vm.at[:, 0:HD], a_all.at[half, pl.ds(source * rows, rows), :],
            a_send.at[0], a_recv.at[half * slots + source], rep, sib,
        ).wait_recv()

    def attend(index, half):
        head = head_of(index, half)
        group = head // (HEADS // KVH)
        lanes = pl.ds(pl.multiple_of(head * HD, 128), HD)
        s = lax.dot_general(
            q_ref[:, lanes], kext[group], (((1,), (1,)), ((), ())),
            preferred_element_type=F32,
        ) + bias[...]
        top = jnp.max(s, axis=-1, keepdims=True)
        p = jnp.exp2((s - top) * SCALE).astype(BF16)
        o = jnp.dot(p, vext[group], preferred_element_type=F32)
        mixed = (o[:, 0:HD] / o[:, HD:2 * HD]).astype(BF16)
        attn_vm[:, lanes] = mixed
        if index == slots - 1:
            a_all[half, pl.ds(slot * rows, rows), :] = mixed
        else:
            a_copy(index, half).start()

    def p_copy(step, half):
        to = lax.rem(me + step, n_shard)
        return remote(
            p_out.at[half, pl.ds(pl.multiple_of(to * out_rows, 16), out_rows), :],
            z_in.at[half, me], p_send.at[half * n_shard + step],
            p_recv.at[half * n_shard + me], rep, to,
        )

    def p_arrived(source, half):
        remote(
            p_out.at[half, 0:out_rows, :], z_in.at[half, source], p_send.at[0],
            p_recv.at[half * n_shard + source], rep, sib,
        ).wait_recv()

    def term(half):
        for step in range(1, n_rep):
            for side in range(2):
                a_arrived(rep_at(n_rep - step) * 2 + side, half)
        a_arrived(sib_slot, half)
        p_out[half] = jnp.dot(gt[...], a_all[half], preferred_element_type=F32).astype(BF16)
        for step in range(1, n_shard):
            p_copy(step, half).start()
        z_in[half, me] = p_out[half, pl.ds(pl.multiple_of(me * out_rows, 16), out_rows), :]

    def o_copy(step, half):
        return remote(
            o_all.at[half, rep], o_all.at[half, rep], o_send.at[half * n_rep + step],
            o_recv.at[half * n_rep + rep], rep_at(step), me,
        )

    def share(half):
        for step in range(1, n_shard):
            p_arrived(lax.rem(me + step, n_shard), half)
        for side in range(2):
            total = z_in[half, side].astype(F32)
            for source in range(1, n_chip):
                total = total + z_in[half, 2 * source + side].astype(F32)
            o_all[half, rep, :, side * HD:(side + 1) * HD] = total.astype(BF16)
        for step in range(1, n_rep):
            o_copy(step, half).start()

    def finish(half):
        for step in range(1, n_rep):
            source = rep_at(step)
            remote(
                o_all.at[half, source], o_all.at[half, source], o_send.at[0],
                o_recv.at[half * n_rep + source], rep, sib,
            ).wait_recv()
        for source in range(n_rep):
            for side in range(2):
                at = (source * heads_each + side * halves + half) * HD
                gw_ref[:, at:at + HD] = o_all[half, source, :, side * HD:(side + 1) * HD]

    for half in range(halves):
        for index in range(slots):
            attend(index, half)
            if half == 0 and index >= slots - n_rep + 1:
                step = index - (slots - n_rep)
                g_arrived(rep_at(n_rep - step) * 2 + core)
                g_hand(step).start()
            if half > 0 and index == EARLY:
                if half == 1:
                    g_rest()
                term(half - 1)
    if halves == 1:
        g_rest()
    term(halves - 1)
    out_copy = pltpu.make_async_copy(attn_vm, attn_hbm, out_sem)
    out_copy.start()
    for half in range(halves):
        share(half)
    for half in range(halves):
        finish(half)

    out_copy.wait()
    for d in range(1, reach + 1):
        @pl.when(chip + d < n_chip)
        def _(d=d):
            along(d).wait_send()

        @pl.when(across_exists(d))
        def _(d=d):
            across(d).wait_send()
    for step in range(n_rep):
        g_copy(step).wait_send()
        if step > 0:
            g_hand(step).wait_send()
    for half in range(halves):
        for index in range(slots - 1):
            a_copy(index, half).wait_send()
        for step in range(1, n_shard):
            p_copy(step, half).wait_send()
        for step in range(1, n_rep):
            o_copy(step, half).wait_send()


def local_narrow(queries, keys, values, segments, grad_output):
    n_rep, n_shard = lax.axis_size("rep"), lax.axis_size("shard")
    rows = queries.shape[1]
    span = MOST // rows
    reach = span // 2
    n_chip = n_shard // 2
    features = grad_output.shape[2]
    out_rows = features // n_shard
    width = HEADS * HD // n_rep
    vmem = pl.BlockSpec(memory_space=pltpu.VMEM)
    dma = pltpu.SemaphoreType.DMA
    attn, grad_weight = pl.pallas_call(
        functools.partial(kernel_narrow, n_rep, n_shard),
        out_shape=(
            jax.ShapeDtypeStruct((rows, HEADS * HD), BF16),
            jax.ShapeDtypeStruct((out_rows, HEADS * HD), F32),
        ),
        in_specs=[pl.BlockSpec(memory_space=pltpu.HBM)] * 5,
        out_specs=(vmem, vmem),
        scratch_shapes=[
            pltpu.VMEM((rows, HEADS * HD), BF16),
            pltpu.VMEM((1, rows), jnp.int32),
            pltpu.VMEM((rows, features), BF16),
            dma((5,)),
            pltpu.VMEM((span + 1, rows + 16, 2 * KVH * HD), BF16),
            pltpu.VMEM((KVH, (span + 1) * rows, HD), BF16),
            pltpu.VMEM((KVH, (span + 1) * rows, 2 * HD), BF16),
            pltpu.VMEM((rows, (span + 1) * rows), F32),
            pltpu.VMEM((2, features // 2, rows), BF16),
            pltpu.VMEM((features // 2, 2 * n_rep * rows), BF16),
            pltpu.VMEM((2 * n_rep * rows, width), BF16),
            pltpu.VMEM((n_chip, out_rows, width), BF16),
            pltpu.VMEM((n_chip, out_rows, width), BF16),
            pltpu.VMEM((n_rep, out_rows, width), BF16),
            dma((reach,)), dma((reach,)), dma((reach,)), dma((reach,)),
            dma((2 * n_rep,)), dma((2 * n_rep,)), dma((2 * n_rep,)), dma((2 * n_rep,)),
            dma((n_chip,)), dma((n_chip,)), dma((n_rep,)), dma((n_rep,)),
        ],
        compiler_params=pltpu.CompilerParams(
            collective_id=0, has_side_effects=True, vmem_limit_bytes=63 * 1024 * 1024
        ),
    )(queries[0], keys[0], values[0], segments, grad_output[0])
    return attn[None], grad_weight


def local_wide(queries, keys, values, segments, grad_output):
    n_rep, n_shard = lax.axis_size("rep"), lax.axis_size("shard")
    rows = queries.shape[1]
    span = MOST // rows
    reach = span // 2
    features = grad_output.shape[2]
    out_rows = features // n_shard
    slots = 2 * n_rep
    halves = HEADS // slots
    vmem = pl.BlockSpec(memory_space=pltpu.VMEM)
    dma = pltpu.SemaphoreType.DMA
    attn, grad_weight = pl.pallas_call(
        functools.partial(kernel, n_rep, n_shard),
        out_shape=(
            jax.ShapeDtypeStruct((rows, HEADS * HD), BF16),
            jax.ShapeDtypeStruct((out_rows, HEADS * HD), BF16),
        ),
        in_specs=[pl.BlockSpec(memory_space=pltpu.HBM)] * 5,
        out_specs=(pl.BlockSpec(memory_space=pltpu.HBM), vmem),
        scratch_shapes=[
            pltpu.VMEM((rows, HEADS * HD), BF16),
            pltpu.VMEM((1, rows), jnp.int32),
            pltpu.VMEM((rows, features), BF16),
            dma((5,)),
            pltpu.VMEM((span + 1, rows + 16, 2 * KVH * HD), BF16),
            pltpu.VMEM((KVH, (span + 1) * rows, HD), BF16),
            pltpu.VMEM((KVH, (span + 1) * rows, 2 * HD), BF16),
            pltpu.VMEM((rows, (span + 1) * rows), F32),
            pltpu.VMEM((features, rows), BF16),
            pltpu.VMEM((features, slots * rows), BF16),
            pltpu.VMEM((rows, HEADS * HD), BF16),
            pltpu.VMEM((halves, slots * rows, HD), BF16),
            pltpu.VMEM((halves, features, HD), BF16),
            pltpu.VMEM((halves, n_shard, out_rows, HD), BF16),
            pltpu.VMEM((halves, n_rep, out_rows, 2 * HD), BF16),
            dma((reach,)), dma((reach,)), dma((reach,)), dma((reach,)),
            dma((n_rep,)), dma((slots,)), dma((halves * slots,)), dma((halves * slots,)),
            dma((halves * n_shard,)), dma((halves * n_shard,)),
            dma((halves * n_rep,)), dma((halves * n_rep,)), dma((n_rep,)), dma(()),
        ],
        compiler_params=pltpu.CompilerParams(
            collective_id=1, has_side_effects=True, vmem_limit_bytes=63 * 1024 * 1024
        ),
    )(queries[0], keys[0], values[0], segments, grad_output[0])
    return attn[None], grad_weight.astype(F32)


def local(*blocks):
    if HEADS % (2 * lax.axis_size("rep")) == 0:
        return local_wide(*blocks)
    return local_narrow(*blocks)


def solution(mesh):
    placed = (
        P("rep", "shard", None),
        P("rep", "shard", None),
        P("rep", "shard", None),
        P("rep", "shard"),
        P("rep", "shard", None),
    )
    return jax.shard_map(
        local,
        mesh=mesh,
        in_specs=placed,
        out_specs=(P("rep", "shard", None), P("shard", None)),
        check_vma=False,
    )
```
